32 devices in a mesh: space: 4 (over z), work: 8 (over y, x, core).
Axes of the slice: x: 2, y: 2, z: 4, core: 2. Of those that a mesh axis runs over, the one named last changes fastest.
Arguments:
- positions: float32 [3, 32768], P(None, ('space', 'work')), may hold values from -3 to 3
- velocities: float32 [3, 32768], P(None, ('space', 'work')), may hold values from -2 to 2
- masses: float32 [32768], P(('space', 'work')), may hold values from 0.001 to 0.01
- sound2: float32 [32768], P(('space', 'work')), may hold values from 0.1 to 1
- ghost_list: int32 [128, 2], P(('space', 'work')), may hold values from 0 to 7
- dens_list: int32 [256, 6], P(('space', 'work')), may hold values from 0 to 15
- pair_dest: int32 [512, 1], P(('space', 'work')), may hold values from 0 to 7; in each aligned block of 16 rows (0 to 15, 16 to 31, ...) at most 4 rows name the same one
- pair_tiles: int32 [512, 2], P(('space', 'work')), may hold values from 0 to 7
Outputs:
- new_positions: float32 [3, 32768], P(None, ('space', 'work'))
- new_velocities: float32 [3, 32768], P(None, ('space', 'work'))
- acceleration: float32 [3, 32768], P(None, ('space', 'work'))
- density: float32 [32768], P(('space', 'work'))
The draws below stay inside these ranges and needn't reach their ends.
Inputs may be any that keep to these rules, and one draw needn't show every extreme that they name: `pair_dest`: at most 4 pairs of one device name the same owner; in every draw some device has exactly 4 pairs for one owner.
All inputs are finite; a program needn't handle non-finite values.
Results may differ from the reference program's by a relative error of at most 0.0001.
Values sent between devices are 32-bit elements; how exact they have to be, the bound alone decides.
A program may use at most 64 MiB of HBM per device.

```python
import math
import jax
import jax.numpy as jnp
import numpy as np
from jax import lax

TD = 8
G = 4
NBD = 6
PAIRS_DEV = 16
CAP = 4
STEPS = 2
TILES = 256
NPART = 32768
PAIRS = 512
GHOSTS = 128
N_SPACE = 4
N_WORK = 8


def set_ends(array, own_key, low, high):
    dims = array.shape
    spot = [jax.random.randint(jax.random.fold_in(own_key, axis), (), 0, dims[axis]) for axis in range(len(dims))]
    array = array.at[tuple(spot)].set(low)
    longest = dims.index(max(dims))
    spot[longest] = (spot[longest] + 1) % dims[longest]
    return array.at[tuple(spot)].set(high)


def block_scale(stream_key, extent, pieces, least, largest):
    def one(dim, parts):
        steps = jax.random.uniform(jax.random.fold_in(jax.random.fold_in(stream_key, 6), dim), (parts,), jnp.float32, least / len(pieces), largest / len(pieces))
        return jnp.repeat(jnp.exp(steps), extent[dim] // parts).reshape((-1,) + (1,) * (len(extent) - dim - 1))

    loudness = one(*pieces[0])
    for cut in pieces[1:]:
        loudness = loudness * one(*cut)
    return loudness


def assign_block(rng, own, number, rows, number_of, top, limit, lean):
    ranking = jax.random.permutation(rng, number_of)
    crowded, usual = shares(number_of, rows * top, limit, lean, True), shares(number_of, rows * top, limit, lean, False)
    places = jnp.arange(number_of)

    def named(tallies, turn):
        used = int((tallies > 0).sum())
        fixed = max(1, used // 4)
        passed = fixed + (places - fixed + turn * (used - fixed)) % max(1, number_of - fixed)
        return jnp.zeros((number_of,), jnp.int32).at[ranking[jnp.where(places < fixed, places, passed)]].set(jnp.asarray(tallies, jnp.int32))

    tallies = jnp.where(number % 4 == 0, named(crowded, number // 4), named(usual, number - number // 4 - 1))
    mixed = jax.random.permutation(jax.random.fold_in(own, 3), number_of)
    source_of, taker = mixed[0:number_of // 2 * 2:2], mixed[1:number_of // 2 * 2:2]
    room = jnp.minimum(tallies[source_of] - 1, limit - tallies[taker]) // 2
    room = jnp.where((source_of == ranking[0]) | (taker == ranking[0]) | (tallies[taker] == 0), 0, jnp.maximum(room, 0))
    passed = jax.random.randint(jax.random.fold_in(own, 4), (number_of // 2,), 0, 1 << 20) % (room + 1)
    tallies = tallies.at[source_of].add(-passed).at[taker].add(passed)
    members = jnp.searchsorted(jnp.cumsum(tallies), jnp.arange(rows * top), side="right").astype(jnp.int32)
    table = members.reshape(top, rows).T
    table = table[jax.random.permutation(jax.random.fold_in(own, 1), rows)]
    turn = jax.random.randint(jax.random.fold_in(own, 2), (rows, 1), 0, top)
    return jnp.take_along_axis(table, (jnp.arange(top)[None, :] + turn) % top, axis=1)


def shares(amount, total, limit, skew, full):
    loads = [(1 << 20) // math.isqrt(rank ** skew) + 1 for rank in range(1, amount + 1)]
    largest = limit if full else min(limit, max(-(-total // amount), total * loads[0] // sum(loads)))
    least = 1 if total - largest >= amount - 1 else 0
    holding, surplus = [largest] + [least] * (amount - 1), total - largest - least * (amount - 1)
    while surplus > 0:
        free = [i for i in range(1, amount) if holding[i] < largest] or [i for i in range(1, amount) if holding[i] < limit]
        pool, left = sum([loads[i] for i in free]), surplus
        for i in free:
            addition = min(limit - holding[i], max(1, left * loads[i] // pool), surplus)
            holding[i] = holding[i] + addition
            surplus = surplus - addition
    return np.array(holding)


def scatter_about(stream_key, shape, spread, most, pieces=(), held_as=jnp.bfloat16):
    entries = jax.random.normal(stream_key, shape, jnp.float32) * spread
    if len(pieces) > 0:
        entries = block_scale(stream_key, shape, pieces, -0.22, 0.18) * entries
    return jnp.clip(entries, min=-most, max=most).astype(held_as)


def setup_inputs(seed: int = 0) -> dict:
    splits = jax.random.split(jax.random.key(seed), 9)
    positions = scatter_about(splits[0], (3, NPART), 0.5, 3.0, ((1, 32),), jnp.float32)
    velocities = scatter_about(splits[1], (3, NPART), 0.3, 2.0, ((1, 32),), jnp.float32)
    masses = jnp.clip(jnp.exp(math.log(0.01) - 2.30258502 * jax.random.uniform(splits[2], (NPART,), jnp.float32) ** block_scale(splits[2], (NPART,), ((0, 32),), -0.2, 0.2)), 0.001, 0.01)
    sound2 = jnp.clip(jnp.exp(math.log(1.0) - 2.3025851 * jax.random.uniform(splits[3], (NPART,), jnp.float32) ** block_scale(splits[3], (NPART,), ((0, 32),), -0.2, 0.2)), 0.1, 1.0)
    ghost_list = set_ends(jax.random.randint(splits[4], (GHOSTS, 2), 0, TD), jax.random.fold_in(splits[4], 1), 0, TD - 1).astype(jnp.int32)
    dens_list = set_ends(jax.random.randint(splits[5], (TILES, NBD), 0, TD + 2 * G), jax.random.fold_in(splits[5], 1), 0, (TD + 2 * G) - 1).astype(jnp.int32)
    pair_dest_keys = jax.random.split(jax.random.fold_in(splits[6], 1), PAIRS // PAIRS_DEV)
    pair_dest_turns = jax.random.permutation(jax.random.fold_in(splits[6], 3), PAIRS // PAIRS_DEV)
    pair_dest = jax.vmap(lambda own, number: assign_block(jax.random.fold_in(splits[6], 2), own, number, PAIRS_DEV, N_WORK, 1, CAP, 2))(pair_dest_keys, pair_dest_turns).reshape((PAIRS, 1))
    pair_tiles = set_ends(jax.random.randint(splits[7], (PAIRS, 2), 0, TD), jax.random.fold_in(splits[7], 1), 0, TD - 1).astype(jnp.int32)
    return {"positions": positions, "velocities": velocities, "masses": masses, "sound2": sound2, "ghost_list": ghost_list, "dens_list": dens_list, "pair_dest": pair_dest, "pair_tiles": pair_tiles}


kernel_scale = 1.0
viscous_alpha = 1.0
viscous_beta = 2.0
star_mass = 0.5
softening = 0.1
time_step = 0.1

def tile_density(home_tile, neighbours):
    combined = jnp.concatenate([home_tile[None], neighbours], axis=0)
    combined = jnp.transpose(combined, (1, 0, 2)).reshape(4, -1)
    distance2 = jnp.zeros((home_tile.shape[1], combined.shape[1]), jnp.float32)
    for k in range(3):
        offset = home_tile[k][:, None] - combined[k][None, :]
        distance2 = distance2 + offset * offset
    kernel = jnp.exp(-distance2 * kernel_scale)
    return lax.optimization_barrier(jnp.sum(kernel * combined[3][None, :], axis=1))

def pair_terms(first_tile, second_tile):
    offsets = first_tile[0:3, :, None] - second_tile[0:3, None, :]
    distance2 = lax.optimization_barrier(jnp.sum(offsets * offsets, axis=0))
    velocity_gap = first_tile[3:6, :, None] - second_tile[3:6, None, :]
    approach = lax.optimization_barrier(jnp.sum(velocity_gap * offsets, axis=0))
    closing = jnp.minimum(approach / (distance2 + 0.01), 0.0)
    mean_sound = 0.5 * (first_tile[9][:, None] + second_tile[9][None, :])
    mean_density = 0.5 * (first_tile[7][:, None] + second_tile[7][None, :])
    viscous = (-viscous_alpha * mean_sound * closing + viscous_beta * closing * closing) / mean_density
    strength = first_tile[8][:, None] + second_tile[8][None, :] + viscous
    weight = strength * jnp.exp(-distance2 * kernel_scale) * (2.0 * kernel_scale)
    on_first = lax.optimization_barrier(jnp.sum(weight[None] * second_tile[6][None, None, :] * offsets, axis=2))
    on_second = -lax.optimization_barrier(jnp.sum(weight[None] * first_tile[6][None, :, None] * offsets, axis=1))
    return (on_first, on_second)

def star_pull(positions):
    radius2 = lax.optimization_barrier(jnp.sum(positions * positions, axis=0)) + softening
    return -star_mass * positions / (radius2 * jnp.sqrt(radius2))[None, :]

def reference(positions, velocities, masses, sound2, ghost_list, dens_list, pair_dest, pair_tiles):
    device_total = N_SPACE * N_WORK
    tile_total = device_total * TD
    pair_total = device_total * PAIRS_DEV
    per_block = 16
    device_ids = jnp.arange(device_total, dtype=jnp.int32)
    sector = device_ids // N_WORK
    work_place = device_ids % N_WORK
    lower_device = (sector - 1) % N_SPACE * N_WORK + work_place
    upper_device = (sector + 1) % N_SPACE * N_WORK + work_place
    ghosts = ghost_list.reshape(device_total, G, 2)
    own_ids = device_ids[:, None] * TD + jnp.arange(TD, dtype=jnp.int32)[None, :]
    from_below = lower_device[:, None] * TD + ghosts[lower_device][:, :, 0]
    from_above = upper_device[:, None] * TD + ghosts[upper_device][:, :, 1]
    candidates = jnp.concatenate([own_ids, from_below, from_above], axis=1)
    tile_device = jnp.arange(tile_total, dtype=jnp.int32) // TD
    density_tiles = candidates[tile_device[:, None], dens_list]
    pair_device = jnp.arange(pair_total, dtype=jnp.int32) // PAIRS_DEV
    first_ids = pair_device * TD + pair_tiles[:, 0]
    second_ids = (pair_device - pair_device % N_WORK + pair_dest[:, 0]) * TD + pair_tiles[:, 1]
    tile_mass = masses.reshape(tile_total, 1, 128)
    sound_speed = jnp.sqrt(sound2).reshape(tile_total, 1, 128)
    acceleration = jnp.zeros_like(positions)
    density = jnp.zeros_like(masses)
    for _ in range(STEPS):
        tile_pos = jnp.transpose(positions.reshape(3, tile_total, 128), (1, 0, 2))
        tile_vel = jnp.transpose(velocities.reshape(3, tile_total, 128), (1, 0, 2))
        source = jnp.concatenate([tile_pos, tile_mass], axis=1)

        def density_block(indices):
            return jax.vmap(tile_density)(source[indices[0]], source[indices[1]])
        density = lax.map(density_block, (jnp.arange(tile_total, dtype=jnp.int32).reshape(-1, per_block), density_tiles.reshape(-1, per_block, NBD))).reshape(-1)
        pressure_term = (sound2 / density).reshape(tile_total, 1, 128)
        payload = jnp.concatenate([tile_pos, tile_vel, tile_mass, density.reshape(tile_total, 1, 128), pressure_term, sound_speed], axis=1)

        def pair_block(indices):
            return jax.vmap(pair_terms)(payload[indices[0]], payload[indices[1]])
        on_first, on_second = lax.map(pair_block, (first_ids.reshape(-1, per_block), second_ids.reshape(-1, per_block)))
        pair_gains = jnp.zeros((tile_total, 3, 128), jnp.float32)
        pair_gains = pair_gains.at[first_ids].add(on_first.reshape(-1, 3, 128))
        pair_gains = pair_gains.at[second_ids].add(on_second.reshape(-1, 3, 128))
        acceleration = jnp.transpose(pair_gains, (1, 0, 2)).reshape(3, -1) + star_pull(positions)
        velocities = velocities + time_step * acceleration
        positions = positions + time_step * velocities
    return (positions, velocities, acceleration, density)
```

```python
import functools

import jax
import jax.numpy as jnp
from jax import lax
from jax.experimental import pallas as pl
from jax.experimental.pallas import tpu as pltpu
from jax.sharding import PartitionSpec as P

STEPS = 2
MESH = pl.DeviceIdType.MESH
NT = (((1,), (1,)), ((), ()))
NN = (((1,), (0,)), ((), ()))
TN = (((0,), (0,)), ((), ()))
HIGHEST = lax.Precision.HIGHEST

star_mass = 0.5
softening = 0.1
time_step = 0.1


def inverse(value):
    guess = pl.reciprocal(value, approx=True)
    return guess * (2.0 - value * guess)


def halves(value):
    high = value.astype(jnp.bfloat16)
    return high, (value - high.astype(jnp.float32)).astype(jnp.bfloat16)


def thirds(value):
    high = value.astype(jnp.bfloat16).astype(jnp.float32)
    rest = value - high
    middle = rest.astype(jnp.bfloat16).astype(jnp.float32)
    return jnp.concatenate([high, middle, rest - middle], axis=0).astype(jnp.bfloat16)


def moment_rows(position_rows, mass_row):
    rows = [mass_row] + [mass_row * row for row in position_rows]
    return thirds(jnp.concatenate(rows, axis=0))


def kernel(
    work, space,
    pos, vel, mass, snd, ghost, dens, dest_s, tiles_s, dest_v, tiles_v,
    new_pos, new_vel, acc_out, den_out,
    spread, spread_rho, cand, factors, on_first, on_second,
    sector0, sector1, rho0, rho1, ghosts_out0, ghosts_out1, ghosts_in0, ghosts_in1,
    react_out0, react_out1, react_in0, react_in1,
    send_sem, recv_sem, ghost_send, ghost_recv,
):
    tiles = mass.shape[0]
    pairs = dest_v.shape[0]
    ghost_count = ghost.shape[0]
    listed = dens.shape[1]
    me = lax.axis_index("work")
    here = lax.axis_index("space")
    above, below = lax.rem(here + 1, space), lax.rem(here + space - 1, space)

    barrier = pltpu.get_barrier_semaphore()
    for s in range(1, work):
        pl.semaphore_signal(
            barrier, inc=1, device_id={"work": lax.rem(me + s, work)}, device_id_type=MESH
        )
    for z in (above, below):
        pl.semaphore_signal(barrier, inc=1, device_id={"space": z}, device_id_type=MESH)

    def everyone(step, kind, source, target, own_slot):
        copies = []
        for s in range(1, work):
            to, origin = lax.rem(me + s, work), lax.rem(me + work - s, work)
            if own_slot:
                out, into, arriving = source.at[me], target.at[me], target.at[origin]
            else:
                out, into, arriving = source.at[to], target.at[me], target.at[origin]
            sems = (send_sem.at[step, kind, s - 1], recv_sem.at[step, kind, s - 1])
            copy = pltpu.make_async_remote_copy(
                src_ref=out, dst_ref=into, send_sem=sems[0], recv_sem=sems[1],
                device_id={"work": to}, device_id_type=MESH,
            )
            arrival = pltpu.make_async_remote_copy(
                src_ref=arriving, dst_ref=arriving, send_sem=sems[0], recv_sem=sems[1],
                device_id={"work": to}, device_id_type=MESH,
            )
            copies.append((copy, arrival))
        return copies

    masses = mass[...]
    sound2 = snd[...]
    sound = jnp.sqrt(sound2)
    positions, velocities = [], []
    for k in range(3):
        positions.append(
            jnp.concatenate([pos[k : k + 1, 128 * t : 128 * t + 128] for t in range(tiles)], axis=0)
        )
        velocities.append(
            jnp.concatenate([vel[k : k + 1, 128 * t : 128 * t + 128] for t in range(tiles)], axis=0)
        )
    owner_hits = (
        lax.broadcasted_iota(jnp.int32, (pairs, work * tiles), 1)
        == dest_v[...] * tiles + tiles_v[:, 1:2]
    ).astype(jnp.float32)
    first_hits = (
        lax.broadcasted_iota(jnp.int32, (pairs, tiles), 1) == tiles_v[:, 0:1]
    ).astype(jnp.float32)

    sectors, rhos = (sector0, sector1), (rho0, rho1)
    ghosts_outs, ghosts_ins = (ghosts_out0, ghosts_out1), (ghosts_in0, ghosts_in1)
    react_outs, react_ins = (react_out0, react_out1), (react_in0, react_in1)
    pending = []
    acceleration, density = None, None
    for step in range(STEPS):
        sector, rho, react_out, react_in = sectors[step], rhos[step], react_outs[step], react_ins[step]
        ghosts_out, ghosts_in = ghosts_outs[step], ghosts_ins[step]

        for k in range(3):
            cand[k, 0:tiles, :] = positions[k]
            sector[me, k] = positions[k]
            sector[me, 3 + k] = velocities[k]
        if step == 0:
            cand[3, 0:tiles, :] = masses
            sector[me, 6] = masses
            sector[me, 7] = sound
        for way in range(2):
            for j in range(ghost_count):
                number = ghost[j, way]
                for k in range(4):
                    ghosts_out[way, k * ghost_count + j : k * ghost_count + j + 1, :] = cand[
                        k, pl.ds(number, 1), :
                    ]
        if step == 0:
            pl.semaphore_wait(barrier, work + 1)
        ghost_copies = []
        for way, z in enumerate((above, below)):
            copy = pltpu.make_async_remote_copy(
                src_ref=ghosts_out.at[way], dst_ref=ghosts_in.at[way],
                send_sem=ghost_send.at[step, way], recv_sem=ghost_recv.at[step, way],
                device_id={"space": z}, device_id_type=MESH,
            )
            copy.start()
            ghost_copies.append(copy)
        sector_copies = everyone(step, 0, sector, sector, True)
        for copy, _ in sector_copies:
            copy.start()

        planes = positions + velocities + ([sound] if step == 0 else [])
        blank = jnp.zeros((128 - tiles * len(planes), 128), jnp.float32)
        columns = jnp.concatenate(planes + [blank], axis=0).T
        for q in range(len(planes)):
            for t in range(tiles):
                c = q * tiles + t
                spread[t, q] = jnp.broadcast_to(columns[:, c : c + 1], (128, 128))

        for copy in ghost_copies:
            copy.wait_recv()
        for way in range(2):
            first = tiles + way * ghost_count
            for k in range(4):
                cand[k, first : first + ghost_count, :] = ghosts_in[
                    way, k * ghost_count : (k + 1) * ghost_count, :
                ]

        def density_of(t, carry):
            rows = []
            for c in range(listed + 1):
                number = t if c == 0 else dens[t, c - 1]
                rows.append([cand[k, pl.ds(number, 1), :] for k in range(4)])
            total = []
            for i in range(0, 128, 32):
                home = [spread[t, k, i : i + 32, :] for k in range(3)]
                part = jnp.zeros((32, 128), jnp.float32)
                for row in rows:
                    gaps = [home[k] - row[k] for k in range(3)]
                    distance2 = gaps[0] * gaps[0] + gaps[1] * gaps[1] + gaps[2] * gaps[2]
                    part = part + jnp.exp(-distance2) * row[3]
                total.append(part)
            high, low = halves(jnp.concatenate(total, axis=0))
            ones = jnp.ones((8, 256), jnp.bfloat16)
            sums = lax.dot_general(
                ones, jnp.concatenate([high, low], axis=1), NT, preferred_element_type=jnp.float32
            )
            rho[me, 0, pl.ds(t, 1), :] = sums[0:1, :]
            return carry

        lax.fori_loop(0, tiles, density_of, 0)
        density = rho[me, 0]
        pressure = sound2 / density
        rho[me, 1] = pressure
        rho_copies = everyone(step, 1, rho, rho, True)
        for copy, _ in rho_copies:
            copy.start()
        blank = jnp.zeros((128 - 2 * tiles, 128), jnp.float32)
        columns = jnp.concatenate([density, pressure, blank], axis=0).T
        for q in range(2):
            for t in range(tiles):
                c = q * tiles + t
                spread_rho[t, q] = jnp.broadcast_to(columns[:, c : c + 1], (128, 128))

        for _, arrival in sector_copies:
            arrival.wait_recv()

        def pair_factors(p, carry):
            a, owner, b = tiles_s[p, 0], dest_s[p, 0], tiles_s[p, 1]
            row = [sector[owner, k, pl.ds(b, 1), :] for k in range(6)]
            row_sound = sector0[owner, 7, pl.ds(b, 1), :]
            for i in range(0, 128, 32):
                home = [spread[a, k, i : i + 32, :] for k in range(7)]
                gaps = [home[k] - row[k] for k in range(3)]
                distance2 = gaps[0] * gaps[0] + gaps[1] * gaps[1] + gaps[2] * gaps[2]
                approach = (home[3] - row[3]) * gaps[0]
                approach = approach + (home[4] - row[4]) * gaps[1]
                approach = approach + (home[5] - row[5]) * gaps[2]
                closing = jnp.minimum(approach * inverse(distance2 + 0.01), 0.0)
                twice = 2.0 * jnp.exp(-distance2)
                factors[p, 0, i : i + 32, :] = twice
                factors[p, 1, i : i + 32, :] = (
                    twice * closing * (4.0 * closing - (home[6] + row_sound))
                )
            return carry

        lax.fori_loop(0, pairs, pair_factors, 0)
        for _, arrival in rho_copies:
            arrival.wait_recv()

        def pair_gains(p, carry):
            a, owner, b = tiles_s[p, 0], dest_s[p, 0], tiles_s[p, 1]
            row_rho = rho[owner, 0, pl.ds(b, 1), :]
            row_pressure = rho[owner, 1, pl.ds(b, 1), :]
            weight = factors[p, 0] * (spread_rho[a, 1] + row_pressure) + factors[p, 1] * inverse(
                spread_rho[a, 0] + row_rho
            )
            high, low = halves(weight)
            first_rows = [sector[me, k, pl.ds(a, 1), :] for k in range(3)]
            second_rows = [sector[owner, k, pl.ds(b, 1), :] for k in range(3)]
            first_moments = moment_rows(first_rows, sector0[me, 6, pl.ds(a, 1), :])
            second_moments = moment_rows(second_rows, sector0[owner, 6, pl.ds(b, 1), :])
            of_second = lax.dot_general(
                jnp.concatenate([second_moments] * 2, axis=1),
                jnp.concatenate([high, low], axis=1),
                NT, preferred_element_type=jnp.float32,
            )
            of_first = lax.dot_general(
                jnp.concatenate([first_moments] * 2, axis=1),
                jnp.concatenate([high, low], axis=0),
                NN, preferred_element_type=jnp.float32,
            )
            of_second = of_second[0:4] + of_second[4:8] + of_second[8:12]
            of_first = of_first[0:4] + of_first[4:8] + of_first[8:12]
            for k in range(3):
                on_first[k, pl.ds(p, 1), :] = (
                    first_rows[k] * of_second[0:1] - of_second[k + 1 : k + 2]
                )
                on_second[k, pl.ds(p, 1), :] = (
                    second_rows[k] * of_first[0:1] - of_first[k + 1 : k + 2]
                )
            return carry

        lax.fori_loop(0, pairs, pair_gains, 0)
        for k in range(3):
            reaction = lax.dot_general(
                owner_hits, on_second[k], TN, precision=HIGHEST,
                preferred_element_type=jnp.float32,
            )
            for w in range(work):
                react_out[w, k] = reaction[w * tiles : (w + 1) * tiles, :]
        react_copies = everyone(step, 2, react_out, react_in, False)
        for copy, _ in react_copies:
            copy.start()
        radius2 = positions[0] * positions[0] + positions[1] * positions[1]
        radius2 = radius2 + positions[2] * positions[2] + softening
        pull = -star_mass / (radius2 * jnp.sqrt(radius2))
        acceleration = []
        for k in range(3):
            gain = lax.dot_general(
                first_hits, on_first[k], TN, precision=HIGHEST, preferred_element_type=jnp.float32
            )
            acceleration.append(gain + pull * positions[k] + react_out[me, k])
        for s, (_, arrival) in enumerate(react_copies):
            arrival.wait_recv()
            origin = lax.rem(me + work - (s + 1), work)
            for k in range(3):
                acceleration[k] = acceleration[k] + react_in[origin, k]
        velocities = [velocities[k] + time_step * acceleration[k] for k in range(3)]
        positions = [positions[k] + time_step * velocities[k] for k in range(3)]
        pending = pending + ghost_copies + [
            copy for copy, _ in sector_copies + rho_copies + react_copies
        ]

    den_out[...] = density
    for k in range(3):
        for t in range(tiles):
            lanes = slice(128 * t, 128 * t + 128)
            new_pos[k : k + 1, lanes] = positions[k][t : t + 1, :]
            new_vel[k : k + 1, lanes] = velocities[k][t : t + 1, :]
            acc_out[k : k + 1, lanes] = acceleration[k][t : t + 1, :]
    for copy in pending:
        copy.wait_send()


def local(positions, velocities, masses, sound2, ghost_list, dens_list, pair_dest, pair_tiles):
    work, space = lax.axis_size("work"), lax.axis_size("space")
    particles = positions.shape[1]
    tiles = particles // 128
    pairs = pair_dest.shape[0]
    ghosts = ghost_list.shape[0]
    vmem = pl.BlockSpec(memory_space=pltpu.VMEM)
    smem = pl.BlockSpec(memory_space=pltpu.SMEM)
    f32 = jnp.float32
    wide = jax.ShapeDtypeStruct((3, particles), f32)
    per_step = []
    for shape0, shape1 in (
        ((work, 8, tiles, 128), (work, 6, tiles, 128)),
        ((work, 2, tiles, 128), (work, 2, tiles, 128)),
        ((2, 4 * ghosts, 128), (2, 4 * ghosts, 128)),
        ((2, 4 * ghosts, 128), (2, 4 * ghosts, 128)),
        ((work, 3, tiles, 128), (work, 3, tiles, 128)),
        ((work, 3, tiles, 128), (work, 3, tiles, 128)),
    ):
        per_step += [pltpu.VMEM(shape0, f32), pltpu.VMEM(shape1, f32)]
    outs = pl.pallas_call(
        functools.partial(kernel, work, space),
        out_shape=(wide, wide, wide, jax.ShapeDtypeStruct((tiles, 128), f32)),
        in_specs=[vmem] * 4 + [smem] * 4 + [vmem] * 2,
        out_specs=(vmem,) * 4,
        scratch_shapes=[
            pltpu.VMEM((tiles, 7, 128, 128), f32),
            pltpu.VMEM((tiles, 2, 128, 128), f32),
            pltpu.VMEM((4, tiles + 2 * ghosts, 128), f32),
            pltpu.VMEM((pairs, 2, 128, 128), f32),
            pltpu.VMEM((3, pairs, 128), f32),
            pltpu.VMEM((3, pairs, 128), f32),
            *per_step,
            pltpu.SemaphoreType.DMA((STEPS, 3, work - 1)),
            pltpu.SemaphoreType.DMA((STEPS, 3, work - 1)),
            pltpu.SemaphoreType.DMA((STEPS, 2)),
            pltpu.SemaphoreType.DMA((STEPS, 2)),
        ],
        compiler_params=pltpu.CompilerParams(
            collective_id=0, has_side_effects=True, vmem_limit_bytes=48 * 1024 * 1024
        ),
        name="leapfrog",
    )(
        positions, velocities, masses.reshape(tiles, 128), sound2.reshape(tiles, 128),
        ghost_list, dens_list, pair_dest, pair_tiles, pair_dest, pair_tiles,
    )
    return outs[0], outs[1], outs[2], outs[3].reshape(particles)


def solution(mesh):
    return jax.shard_map(
        local,
        mesh=mesh,
        in_specs=(
            P(None, ("space", "work")),
            P(None, ("space", "work")),
            P(("space", "work")),
            P(("space", "work")),
            P(("space", "work"), None),
            P(("space", "work"), None),
            P(("space", "work"), None),
            P(("space", "work"), None),
        ),
        out_specs=(
            P(None, ("space", "work")),
            P(None, ("space", "work")),
            P(None, ("space", "work")),
            P(("space", "work")),
        ),
        check_vma=False,
    )
```

```python
import functools
import math

import jax
import jax.numpy as jnp
from jax import lax
from jax.experimental import pallas as pl
from jax.experimental.pallas import tpu as pltpu
from jax.sharding import PartitionSpec as P

STEPS = 2
MESH = pl.DeviceIdType.MESH
NT = (((1,), (1,)), ((), ()))
NN = (((1,), (0,)), ((), ()))
LOG2E = math.log2(math.e)
ROOT_LOG2E = math.sqrt(LOG2E)
HIGHEST = lax.Precision.HIGHEST

star_mass = 0.5
softening = 0.1
time_step = 0.1


def inverse(value):
    guess = pl.reciprocal(value, approx=True)
    return guess * (2.0 - value * guess)


def halves(value):
    high = value.astype(jnp.bfloat16)
    return high, (value - high.astype(jnp.float32)).astype(jnp.bfloat16)


def kernel(
    work, space,
    pos_in, vel_in, mass_in, snd_in, ghost_in, dens_in, dest_in, tiles_in,
    result,
    pos, vel, mass, snd, ghost, dens, dest_s, tiles_s, dest_v, tiles_v, load_sem,
    spread, spread_rho, cand, factors, cand_scaled, totals, weights, gathered, moments, sums,
    sector0, sector1, rho0, rho1, ghosts_out0, ghosts_out1, ghosts_in0, ghosts_in1,
    react_out0, react_out1, react_in0, react_in1,
    send_sem, recv_sem, ghost_send, ghost_recv,
):
    tiles = mass.shape[0]
    pairs = dest_v.shape[1]
    ghost_count = ghost.shape[1]
    listed = dens.shape[1]
    unroll = math.gcd(pairs, 4)
    loads = []
    for n, (source, target) in enumerate((
        (pos_in, pos), (vel_in, vel), (mass_in, mass), (snd_in, snd), (ghost_in, ghost),
        (dens_in, dens), (dest_in, dest_s), (tiles_in, tiles_s), (dest_in, dest_v),
        (tiles_in, tiles_v),
    )):
        copy = pltpu.make_async_copy(source, target, load_sem.at[n])
        copy.start()
        loads.append(copy)
    me = lax.axis_index("work")
    here = lax.axis_index("space")
    above, below = lax.rem(here + 1, space), lax.rem(here + space - 1, space)

    barrier = pltpu.get_barrier_semaphore()
    for s in range(1, work):
        pl.semaphore_signal(
            barrier, inc=1, device_id={"work": lax.rem(me + s, work)}, device_id_type=MESH
        )
    for z in (above, below):
        pl.semaphore_signal(barrier, inc=1, device_id={"space": z}, device_id_type=MESH)

    def everyone(step, kind, source, target, own_slot):
        copies = []
        for s in range(1, work):
            to, origin = lax.rem(me + s, work), lax.rem(me + work - s, work)
            if own_slot:
                out, into, arriving = source.at[me], target.at[me], target.at[origin]
            else:
                out, into, arriving = source.at[to], target.at[me], target.at[origin]
            sems = (send_sem.at[step, kind, s - 1], recv_sem.at[step, kind, s - 1])
            copy = pltpu.make_async_remote_copy(
                src_ref=out, dst_ref=into, send_sem=sems[0], recv_sem=sems[1],
                device_id={"work": to}, device_id_type=MESH,
            )
            arrival = pltpu.make_async_remote_copy(
                src_ref=arriving, dst_ref=arriving, send_sem=sems[0], recv_sem=sems[1],
                device_id={"work": to}, device_id_type=MESH,
            )
            copies.append((copy, arrival))
        return copies

    for copy in loads:
        copy.wait()
    masses = mass[...]
    sound2 = snd[...]
    sound = jnp.sqrt(sound2)
    positions, velocities = [], []
    for k in range(3):
        positions.append(
            jnp.concatenate([pos[k : k + 1, 128 * t : 128 * t + 128] for t in range(tiles)], axis=0)
        )
        velocities.append(
            jnp.concatenate([vel[k : k + 1, 128 * t : 128 * t + 128] for t in range(tiles)], axis=0)
        )
    owner_hits = (
        lax.broadcasted_iota(jnp.int32, (work * tiles, pairs), 0)
        == dest_v[...] * tiles + tiles_v[1:2, :]
    ).astype(jnp.float32)
    first_hits = (
        lax.broadcasted_iota(jnp.int32, (tiles, pairs), 0) == tiles_v[0:1, :]
    ).astype(jnp.float32)

    sectors, rhos = (sector0, sector1), (rho0, rho1)
    ghosts_outs, ghosts_ins = (ghosts_out0, ghosts_out1), (ghosts_in0, ghosts_in1)
    react_outs, react_ins = (react_out0, react_out1), (react_in0, react_in1)
    pending = []
    acceleration, density = None, None
    for step in range(STEPS):
        sector, rho, react_out, react_in = sectors[step], rhos[step], react_outs[step], react_ins[step]
        ghosts_out, ghosts_in = ghosts_outs[step], ghosts_ins[step]

        for k in range(3):
            cand[k, 0:tiles, :] = positions[k]
            sector[me, k] = positions[k]
            sector[me, 3 + k] = velocities[k]
        if step == 0:
            cand[3, 0:tiles, :] = masses
            sector[me, 6] = masses
            sector[me, 7] = sound
        for way in range(2):
            for j in range(ghost_count):
                number = ghost[way, j]
                for k in range(4):
                    ghosts_out[way, k * ghost_count + j : k * ghost_count + j + 1, :] = cand[
                        k, pl.ds(number, 1), :
                    ]
        if step == 0:
            pl.semaphore_wait(barrier, work + 1)
        ghost_copies = []
        for way, z in enumerate((above, below)):
            copy = pltpu.make_async_remote_copy(
                src_ref=ghosts_out.at[way], dst_ref=ghosts_in.at[way],
                send_sem=ghost_send.at[step, way], recv_sem=ghost_recv.at[step, way],
                device_id={"space": z}, device_id_type=MESH,
            )
            copy.start()
            ghost_copies.append(copy)
        sector_copies = everyone(step, 0, sector, sector, True)
        for copy, _ in sector_copies:
            copy.start()

        planes = positions + velocities + ([sound] if step == 0 else [])
        blank = jnp.zeros((128 - tiles * len(planes), 128), jnp.float32)
        columns = jnp.concatenate(planes + [blank], axis=0).T
        for q in range(len(planes)):
            for t in range(tiles):
                c = q * tiles + t
                spread[t, q] = jnp.broadcast_to(columns[:, c : c + 1], (128, 128))

        for copy in ghost_copies:
            copy.wait_recv()
        for way in range(2):
            first = tiles + way * ghost_count
            for k in range(4):
                cand[k, first : first + ghost_count, :] = ghosts_in[
                    way, k * ghost_count : (k + 1) * ghost_count, :
                ]

        scaled = [cand[k] * ROOT_LOG2E for k in range(3)]
        mass_log2 = jnp.log2(cand[3])
        for k in range(3):
            cand_scaled[k] = scaled[k]
        cand_scaled[3] = mass_log2

        def density_of(first, carry):
            for t in [first * 2, first * 2 + 1]:
                rows = []
                for c in range(listed + 1):
                    number = t if c == 0 else dens[t, c - 1]
                    rows.append([
                        jnp.broadcast_to(cand_scaled[k, pl.ds(number, 1), :], (32, 128))
                        for k in range(4)
                    ])
                for i in range(0, 128, 32):
                    home = [spread[t, k, i : i + 32, :] * ROOT_LOG2E for k in range(3)]
                    part = None
                    for row in rows:
                        gaps = [home[k] - row[k] for k in range(3)]
                        distance2 = gaps[0] * gaps[0] + gaps[1] * gaps[1] + gaps[2] * gaps[2]
                        term = jnp.exp2(row[3] - distance2)
                        part = term if part is None else part + term
                    totals[t, i : i + 32, :] = part
            return carry

        lax.fori_loop(0, tiles // 2, density_of, 0)
        high, low = halves(totals[...].reshape(tiles * 128, 128))
        ones = jnp.ones((8, 256), jnp.bfloat16)
        row_sums = lax.dot_general(
            ones, jnp.concatenate([high, low], axis=1), NT, preferred_element_type=jnp.float32
        )
        density = jnp.concatenate(
            [row_sums[0:1, 128 * t : 128 * t + 128] for t in range(tiles)], axis=0
        )
        rho[me, 0] = density
        pressure = sound2 / density
        rho[me, 1] = pressure
        rho_copies = everyone(step, 1, rho, rho, True)
        for copy, _ in rho_copies:
            copy.start()
        blank = jnp.zeros((128 - 2 * tiles, 128), jnp.float32)
        columns = jnp.concatenate([density, pressure, blank], axis=0).T
        for q in range(2):
            for t in range(tiles):
                c = q * tiles + t
                spread_rho[t, q] = jnp.broadcast_to(columns[:, c : c + 1], (128, 128))

        for _, arrival in sector_copies:
            arrival.wait_recv()

        def pair_factors(turn, carry):
            for u in range(unroll):
                p = turn * unroll + u
                a, owner, b = tiles_s[0, p], dest_s[0, p], tiles_s[1, p]
                row = [sector[owner, k, pl.ds(b, 1), :] for k in range(6)]
                for k in range(3):
                    gathered[k, pl.ds(p, 1), :] = sector[me, k, pl.ds(a, 1), :]
                    gathered[4 + k, pl.ds(p, 1), :] = row[k]
                gathered[3, pl.ds(p, 1), :] = sector0[me, 6, pl.ds(a, 1), :]
                gathered[7, pl.ds(p, 1), :] = sector0[owner, 6, pl.ds(b, 1), :]
                row.append(sector0[owner, 7, pl.ds(b, 1), :])
                row = [jnp.broadcast_to(value, (32, 128)) for value in row]
                for i in range(0, 128, 32):
                    home = [spread[a, k, i : i + 32, :] for k in range(7)]
                    gaps = [home[k] - row[k] for k in range(3)]
                    distance2 = gaps[0] * gaps[0] + gaps[1] * gaps[1] + gaps[2] * gaps[2]
                    approach = (home[3] - row[3]) * gaps[0]
                    approach = approach + (home[4] - row[4]) * gaps[1]
                    approach = approach + (home[5] - row[5]) * gaps[2]
                    closing = jnp.minimum(approach * inverse(distance2 + 0.01), 0.0)
                    twice = jnp.exp2(1.0 - distance2 * LOG2E)
                    factors[p, 0, i : i + 32, :] = twice
                    factors[p, 1, i : i + 32, :] = (
                        twice * closing * (4.0 * closing - (home[6] + row[6]))
                    )
            return carry

        lax.fori_loop(0, pairs // unroll, pair_factors, 0)
        for side in range(2):
            mass_rows = gathered[4 * side + 3]
            for k in range(4):
                value = mass_rows if k == 3 else mass_rows * gathered[4 * side + k]
                for g in range(3):
                    piece = value.astype(jnp.bfloat16).astype(jnp.float32)
                    value = value - piece
                    moments[side, pl.ds((4 * g + k) * pairs, pairs), :] = piece
        for _, arrival in rho_copies:
            arrival.wait_recv()

        def own_moments(side, p):
            rows = moments[side, pl.ds(p, 12, stride=pairs), :].astype(jnp.bfloat16)
            return jnp.concatenate([rows, rows], axis=1)

        def gains(side):
            moved = [
                sums[side, pl.ds(k * pairs, pairs), :]
                + sums[side, pl.ds((4 + k) * pairs, pairs), :]
                + sums[side, pl.ds((8 + k) * pairs, pairs), :]
                for k in range(4)
            ]
            return [gathered[4 * side + k] * moved[3] - moved[k] for k in range(3)]

        def pair_weights(turn, carry):
            for u in range(unroll):
                p = turn * unroll + u
                a, owner, b = tiles_s[0, p], dest_s[0, p], tiles_s[1, p]
                row_rho = jnp.broadcast_to(rho[owner, 0, pl.ds(b, 1), :], (32, 128))
                row_pressure = jnp.broadcast_to(rho[owner, 1, pl.ds(b, 1), :], (32, 128))
                parts = []
                for i in range(0, 128, 32):
                    own = pl.ds(i, 32)
                    weight = factors[p, 0, own, :] * (spread_rho[a, 1, own, :] + row_pressure)
                    weight = weight + factors[p, 1, own, :] * inverse(
                        spread_rho[a, 0, own, :] + row_rho
                    )
                    high, low = halves(weight)
                    weights[p, 0, own, :] = high
                    weights[p, 1, own, :] = low
                    parts.append((high, low))
                stacked = jnp.concatenate([h for h, _ in parts] + [l for _, l in parts], axis=0)
                sums[1, pl.ds(p, 12, stride=pairs), :] = lax.dot_general(
                    own_moments(0, p), stacked, NN, preferred_element_type=jnp.float32
                )
            return carry

        def first_sums(turn, carry):
            for u in range(unroll):
                p = turn * unroll + u
                sums[0, pl.ds(p, 12, stride=pairs), :] = lax.dot_general(
                    own_moments(1, p),
                    jnp.concatenate([weights[p, 0], weights[p, 1]], axis=1),
                    NT, preferred_element_type=jnp.float32,
                )
            return carry

        lax.fori_loop(0, pairs // unroll, pair_weights, 0)
        for k, value in enumerate(gains(1)):
            reaction = lax.dot_general(
                owner_hits, value, NN, precision=HIGHEST, preferred_element_type=jnp.float32
            )
            for w in range(work):
                react_out[w, k] = reaction[w * tiles : (w + 1) * tiles, :]
        react_copies = everyone(step, 2, react_out, react_in, False)
        for copy, _ in react_copies:
            copy.start()
        lax.fori_loop(0, pairs // unroll, first_sums, 0)
        radius2 = positions[0] * positions[0] + positions[1] * positions[1]
        radius2 = radius2 + positions[2] * positions[2] + softening
        pull = -star_mass / (radius2 * jnp.sqrt(radius2))
        acceleration = []
        for k, value in enumerate(gains(0)):
            gain = lax.dot_general(
                first_hits, value, NN, precision=HIGHEST, preferred_element_type=jnp.float32
            )
            acceleration.append(gain + pull * positions[k] + react_out[me, k])
        for s, (_, arrival) in enumerate(react_copies):
            arrival.wait_recv()
            origin = lax.rem(me + work - (s + 1), work)
            for k in range(3):
                acceleration[k] = acceleration[k] + react_in[origin, k]
        velocities = [velocities[k] + time_step * acceleration[k] for k in range(3)]
        positions = [positions[k] + time_step * velocities[k] for k in range(3)]
        pending = pending + ghost_copies + [
            copy for copy, _ in sector_copies + rho_copies + react_copies
        ]

    for k in range(3):
        result[k] = positions[k]
        result[3 + k] = velocities[k]
        result[6 + k] = acceleration[k]
    result[9] = density
    for copy in pending:
        copy.wait_send()


def unpack(result, new_pos, new_vel, acc_out, den_out):
    den_out[...] = result[9]
    for n, out in enumerate((new_pos, new_vel, acc_out)):
        for k in range(3):
            for t in range(den_out.shape[0]):
                out[k : k + 1, 128 * t : 128 * t + 128] = result[3 * n + k, t : t + 1, :]


def local(positions, velocities, masses, sound2, ghost_list, dens_list, pair_dest, pair_tiles):
    work, space = lax.axis_size("work"), lax.axis_size("space")
    particles = positions.shape[1]
    tiles = particles // 128
    pairs = pair_dest.shape[0]
    ghosts = ghost_list.shape[0]
    vmem = pl.BlockSpec(memory_space=pltpu.VMEM)
    f32 = jnp.float32
    per_step = []
    for shape0, shape1 in (
        ((work, 8, tiles, 128), (work, 6, tiles, 128)),
        ((work, 2, tiles, 128), (work, 2, tiles, 128)),
        ((2, 4 * ghosts, 128), (2, 4 * ghosts, 128)),
        ((2, 4 * ghosts, 128), (2, 4 * ghosts, 128)),
        ((work, 3, tiles, 128), (work, 3, tiles, 128)),
        ((work, 3, tiles, 128), (work, 3, tiles, 128)),
    ):
        per_step += [pltpu.VMEM(shape0, f32), pltpu.VMEM(shape1, f32)]
    i32 = jnp.int32
    packed = pl.pallas_call(
        functools.partial(kernel, work, space),
        out_shape=jax.ShapeDtypeStruct((10, tiles, 128), f32),
        in_specs=[pl.BlockSpec(memory_space=pltpu.HBM)] * 8,
        out_specs=vmem,
        scratch_shapes=[
            pltpu.VMEM((3, particles), f32),
            pltpu.VMEM((3, particles), f32),
            pltpu.VMEM((tiles, 128), f32),
            pltpu.VMEM((tiles, 128), f32),
            pltpu.SMEM((2, ghosts), i32),
            pltpu.SMEM(dens_list.shape, i32),
            pltpu.SMEM((1, pairs), i32),
            pltpu.SMEM((2, pairs), i32),
            pltpu.VMEM((1, pairs), i32),
            pltpu.VMEM((2, pairs), i32),
            pltpu.SemaphoreType.DMA((10,)),
            pltpu.VMEM((tiles, 7, 128, 128), f32),
            pltpu.VMEM((tiles, 2, 128, 128), f32),
            pltpu.VMEM((4, tiles + 2 * ghosts, 128), f32),
            pltpu.VMEM((pairs, 2, 128, 128), f32),
            pltpu.VMEM((4, tiles + 2 * ghosts, 128), f32),
            pltpu.VMEM((tiles, 128, 128), f32),
            pltpu.VMEM((pairs, 2, 128, 128), jnp.bfloat16),
            pltpu.VMEM((8, pairs, 128), f32),
            pltpu.VMEM((2, 12 * pairs, 128), f32),
            pltpu.VMEM((2, 12 * pairs, 128), f32),
            *per_step,
            pltpu.SemaphoreType.DMA((STEPS, 3, work - 1)),
            pltpu.SemaphoreType.DMA((STEPS, 3, work - 1)),
            pltpu.SemaphoreType.DMA((STEPS, 2)),
            pltpu.SemaphoreType.DMA((STEPS, 2)),
        ],
        compiler_params=pltpu.CompilerParams(
            collective_id=0, has_side_effects=True, vmem_limit_bytes=63 * 1024 * 1024
        ),
        name="leapfrog",
    )(
        positions, velocities, masses.reshape(tiles, 128), sound2.reshape(tiles, 128),
        ghost_list.T, dens_list, pair_dest.T, pair_tiles.T,
    )
    wide = jax.ShapeDtypeStruct((3, particles), f32)
    outs = pl.pallas_call(
        unpack,
        out_shape=(wide, wide, wide, jax.ShapeDtypeStruct((tiles, 128), f32)),
        in_specs=[vmem],
        out_specs=(vmem,) * 4,
        name="unpack",
    )(packed)
    return outs[0], outs[1], outs[2], outs[3].reshape(particles)


def solution(mesh):
    return jax.shard_map(
        local,
        mesh=mesh,
        in_specs=(
            P(None, ("space", "work")),
            P(None, ("space", "work")),
            P(("space", "work")),
            P(("space", "work")),
            P(("space", "work"), None),
            P(("space", "work"), None),
            P(("space", "work"), None),
            P(("space", "work"), None),
        ),
        out_specs=(
            P(None, ("space", "work")),
            P(None, ("space", "work")),
            P(None, ("space", "work")),
            P(("space", "work")),
        ),
        check_vma=False,
    )
```

```python
import functools
import math

import jax
import jax.numpy as jnp
from jax import lax
from jax.experimental import pallas as pl
from jax.experimental.pallas import tpu as pltpu
from jax.sharding import PartitionSpec as P

STEPS = 2
MESH = pl.DeviceIdType.MESH
NT = (((1,), (1,)), ((), ()))
NN = (((1,), (0,)), ((), ()))
LOG2E = math.log2(math.e)
ROOT_LOG2E = math.sqrt(LOG2E)
HIGHEST = lax.Precision.HIGHEST

star_mass = 0.5
softening = 0.1
time_step = 0.1


def inverse(value):
    guess = pl.reciprocal(value, approx=True)
    return guess * (2.0 - value * guess)


def halves(value):
    high = value.astype(jnp.bfloat16)
    return high, (value - high.astype(jnp.float32)).astype(jnp.bfloat16)


def kernel(
    work, space,
    pos_in, vel_in, mass_in, snd_in, ghost_in, dens_in, dest_in, tiles_in,
    result,
    pos, vel, mass, snd, ghost, dens, dest_s, tiles_s, dest_v, tiles_v, load_sem,
    spread, spread_rho, cand, factors, totals, weights, gathered, moments, sums,
    sector, fixed, rho, ghosts_out, ghosts_in, react_out, react_in,
    send_sem, recv_sem, ghost_send, ghost_recv,
):
    tiles = mass.shape[0]
    pairs = dest_v.shape[1]
    ghost_count = ghost.shape[1]
    listed = dens.shape[1]
    unroll = math.gcd(pairs, 4)
    loads = []
    for n, (source, target) in enumerate((
        (pos_in, pos), (vel_in, vel), (mass_in, mass), (snd_in, snd), (ghost_in, ghost),
        (dens_in, dens), (dest_in, dest_s), (tiles_in, tiles_s), (dest_in, dest_v),
        (tiles_in, tiles_v),
    )):
        copy = pltpu.make_async_copy(source, target, load_sem.at[n])
        copy.start()
        loads.append(copy)
    me = lax.axis_index("work")
    here = lax.axis_index("space")
    above, below = lax.rem(here + 1, space), lax.rem(here + space - 1, space)

    barrier = pltpu.get_barrier_semaphore()
    for s in range(1, work):
        pl.semaphore_signal(
            barrier, inc=1, device_id={"work": lax.rem(me + s, work)}, device_id_type=MESH
        )
    for z in (above, below):
        pl.semaphore_signal(barrier, inc=1, device_id={"space": z}, device_id_type=MESH)

    def everyone(kind, source, target, own_slot):
        copies = []
        for s in range(1, work):
            to, origin = lax.rem(me + s, work), lax.rem(me + work - s, work)
            if own_slot:
                out, into, arriving = source.at[me], target.at[me], target.at[origin]
            else:
                out, into, arriving = source.at[to], target.at[me], target.at[origin]
            sems = (send_sem.at[kind, s - 1], recv_sem.at[kind, s - 1])
            copy = pltpu.make_async_remote_copy(
                src_ref=out, dst_ref=into, send_sem=sems[0], recv_sem=sems[1],
                device_id={"work": to}, device_id_type=MESH,
            )
            arrival = pltpu.make_async_remote_copy(
                src_ref=arriving, dst_ref=arriving, send_sem=sems[0], recv_sem=sems[1],
                device_id={"work": to}, device_id_type=MESH,
            )
            copies.append((copy, arrival))
        return copies

    for copy in loads:
        copy.wait()
    masses = mass[...]
    sound2 = snd[...]
    sound = jnp.sqrt(sound2)
    for k in range(3):
        for t in range(tiles):
            result[k, t : t + 1, :] = pos[k : k + 1, 128 * t : 128 * t + 128]
            result[3 + k, t : t + 1, :] = vel[k : k + 1, 128 * t : 128 * t + 128]
    fixed[me, 0] = masses
    fixed[me, 1] = sound
    cand[3, 0:tiles, :] = jnp.log2(masses)
    lanes = lax.broadcasted_iota(jnp.int32, (128, 128), 1)
    owner_hits = (
        lax.broadcasted_iota(jnp.int32, (work * tiles, pairs), 0)
        == dest_v[...] * tiles + tiles_v[1:2, :]
    ).astype(jnp.float32)
    first_hits = (
        lax.broadcasted_iota(jnp.int32, (tiles, pairs), 0) == tiles_v[0:1, :]
    ).astype(jnp.float32)

    fixed_copies = everyone(3, fixed, fixed, True)

    def one_step(step, carry):
        positions = [result[k] for k in range(3)]
        velocities = [result[3 + k] for k in range(3)]
        for k in range(3):
            cand[k, 0:tiles, :] = positions[k] * ROOT_LOG2E
            sector[me, k] = positions[k]
            sector[me, 3 + k] = velocities[k]
        for way in range(2):
            for j in range(ghost_count):
                number = ghost[way, j]
                for k in range(4):
                    ghosts_out[step, way, k * ghost_count + j : k * ghost_count + j + 1, :] = cand[
                        k, pl.ds(number, 1), :
                    ]

        @pl.when(step == 0)
        def _():
            pl.semaphore_wait(barrier, work + 1)

        ghost_copies = []
        for way, z in enumerate((above, below)):
            copy = pltpu.make_async_remote_copy(
                src_ref=ghosts_out.at[step, way], dst_ref=ghosts_in.at[step, way],
                send_sem=ghost_send.at[step, way], recv_sem=ghost_recv.at[step, way],
                device_id={"space": z}, device_id_type=MESH,
            )
            copy.start()
            ghost_copies.append(copy)
        sector_copies = everyone(0, sector, sector, True)
        for copy, _ in sector_copies:
            copy.start()

        @pl.when(step == 0)
        def _():
            for copy, _ in fixed_copies:
                copy.start()

        def gap2(home, row):
            gaps = [home[k] - row[k] for k in range(3)]
            return gaps[0] * gaps[0] + gaps[1] * gaps[1] + gaps[2] * gaps[2]

        def wide_row(number):
            return [
                jnp.broadcast_to(cand[k, pl.ds(number, 1), :], (32, 128)) for k in range(4)
            ]

        planes = positions + velocities + [sound]
        blank = jnp.zeros((128 - tiles * len(planes), 128), jnp.float32)
        columns = jnp.concatenate(planes + [blank], axis=0).T

        def spread_tile(t, carry):
            turned = pltpu.roll(columns, lax.rem(128 - t, 128), 1)
            for q in range(len(planes)):
                spread[t, q] = jnp.broadcast_to(
                    turned[:, q * tiles : q * tiles + 1], (128, 128)
                )
            row = wide_row(t)
            for i in range(0, 128, 32):
                home = [spread[t, k, i : i + 32, :] * ROOT_LOG2E for k in range(3)]
                totals[t, i : i + 32, :] = jnp.exp2(row[3] - gap2(home, row))
            return carry

        lax.fori_loop(0, tiles, spread_tile, 0)
        for copy in ghost_copies:
            copy.wait_recv()
        for way in range(2):
            first = tiles + way * ghost_count
            for k in range(4):
                cand[k, first : first + ghost_count, :] = ghosts_in[
                    step, way, k * ghost_count : (k + 1) * ghost_count, :
                ]

        def density_of(first, carry):
            for t in [first * 2, first * 2 + 1]:
                rows = [wide_row(dens[t, c]) for c in range(listed)]
                for i in range(0, 128, 32):
                    home = [spread[t, k, i : i + 32, :] * ROOT_LOG2E for k in range(3)]
                    part = totals[t, i : i + 32, :]
                    for row in rows:
                        part = part + jnp.exp2(row[3] - gap2(home, row))
                    spread_rho[t, 0, i : i + 32, :] = jnp.broadcast_to(
                        jnp.sum(part, axis=1, keepdims=True), (32, 128)
                    )
            return carry

        lax.fori_loop(0, tiles // 2, density_of, 0)
        columns = jnp.zeros((128, 128), jnp.float32)
        for t in range(tiles):
            columns = jnp.where(lanes == t, spread_rho[t, 0], columns)
        density = columns.T[0:tiles, :]
        result[9] = density
        rho[me, 0] = density
        rho[me, 1] = sound2 / density
        rho_copies = everyone(1, rho, rho, True)
        for copy, _ in rho_copies:
            copy.start()

        def spread_pressure(t, carry):
            speed = spread[t, 6]
            spread_rho[t, 1] = speed * speed * inverse(spread_rho[t, 0])
            return carry

        lax.fori_loop(0, tiles, spread_pressure, 0)

        for _, arrival in sector_copies:
            arrival.wait_recv()

        @pl.when(step == 0)
        def _():
            for _, arrival in fixed_copies:
                arrival.wait_recv()

        def pair_factors(turn, carry):
            for u in range(unroll):
                p = turn * unroll + u
                a, owner, b = tiles_s[0, p], dest_s[0, p], tiles_s[1, p]
                row = [sector[owner, k, pl.ds(b, 1), :] for k in range(6)]
                for k in range(3):
                    gathered[k, pl.ds(p, 1), :] = sector[me, k, pl.ds(a, 1), :]
                    gathered[4 + k, pl.ds(p, 1), :] = row[k]
                gathered[3, pl.ds(p, 1), :] = fixed[me, 0, pl.ds(a, 1), :]
                gathered[7, pl.ds(p, 1), :] = fixed[owner, 0, pl.ds(b, 1), :]
                row.append(fixed[owner, 1, pl.ds(b, 1), :])
                row = [jnp.broadcast_to(value, (32, 128)) for value in row]
                for i in range(0, 128, 32):
                    home = [spread[a, k, i : i + 32, :] for k in range(7)]
                    gaps = [home[k] - row[k] for k in range(3)]
                    distance2 = gaps[0] * gaps[0] + gaps[1] * gaps[1] + gaps[2] * gaps[2]
                    approach = (home[3] - row[3]) * gaps[0]
                    approach = approach + (home[4] - row[4]) * gaps[1]
                    approach = approach + (home[5] - row[5]) * gaps[2]
                    closing = jnp.minimum(approach * inverse(distance2 + 0.01), 0.0)
                    twice = jnp.exp2(1.0 - distance2 * LOG2E)
                    factors[p, 0, i : i + 32, :] = twice
                    factors[p, 1, i : i + 32, :] = (
                        twice * closing * (4.0 * closing - (home[6] + row[6]))
                    )
            return carry

        lax.fori_loop(0, pairs // unroll, pair_factors, 0)
        for side in range(2):
            mass_rows = gathered[4 * side + 3]
            for k in range(4):
                value = mass_rows if k == 3 else mass_rows * gathered[4 * side + k]
                for g in range(3):
                    piece = value.astype(jnp.bfloat16).astype(jnp.float32)
                    value = value - piece
                    moments[side, pl.ds((4 * g + k) * pairs, pairs), :] = piece
        for _, arrival in rho_copies:
            arrival.wait_recv()

        def own_moments(side, p):
            rows = moments[side, pl.ds(p, 12, stride=pairs), :].astype(jnp.bfloat16)
            return jnp.concatenate([rows, rows], axis=1)

        def gains(side):
            moved = [
                sums[side, pl.ds(k * pairs, pairs), :]
                + sums[side, pl.ds((4 + k) * pairs, pairs), :]
                + sums[side, pl.ds((8 + k) * pairs, pairs), :]
                for k in range(4)
            ]
            return [gathered[4 * side + k] * moved[3] - moved[k] for k in range(3)]

        def pair_weights(turn, carry):
            for u in range(unroll):
                p = turn * unroll + u
                a, owner, b = tiles_s[0, p], dest_s[0, p], tiles_s[1, p]
                row_rho = jnp.broadcast_to(rho[owner, 0, pl.ds(b, 1), :], (32, 128))
                row_pressure = jnp.broadcast_to(rho[owner, 1, pl.ds(b, 1), :], (32, 128))
                parts = []
                for i in range(0, 128, 32):
                    own = pl.ds(i, 32)
                    weight = factors[p, 0, own, :] * (spread_rho[a, 1, own, :] + row_pressure)
                    weight = weight + factors[p, 1, own, :] * inverse(
                        spread_rho[a, 0, own, :] + row_rho
                    )
                    high, low = halves(weight)
                    weights[p, 0, own, :] = high
                    weights[p, 1, own, :] = low
                    parts.append((high, low))
                stacked = jnp.concatenate([h for h, _ in parts] + [l for _, l in parts], axis=0)
                sums[1, pl.ds(p, 12, stride=pairs), :] = lax.dot_general(
                    own_moments(0, p), stacked, NN, preferred_element_type=jnp.float32
                )
            return carry

        def first_sums(turn, carry):
            for u in range(unroll):
                p = turn * unroll + u
                sums[0, pl.ds(p, 12, stride=pairs), :] = lax.dot_general(
                    own_moments(1, p),
                    jnp.concatenate([weights[p, 0], weights[p, 1]], axis=1),
                    NT, preferred_element_type=jnp.float32,
                )
            return carry

        lax.fori_loop(0, pairs // unroll, pair_weights, 0)
        for k, value in enumerate(gains(1)):
            reaction = lax.dot_general(
                owner_hits, value, NN, precision=HIGHEST, preferred_element_type=jnp.float32
            )
            for w in range(work):
                react_out[w, k] = reaction[w * tiles : (w + 1) * tiles, :]
        react_copies = everyone(2, react_out, react_in, False)
        for copy, _ in react_copies:
            copy.start()
        lax.fori_loop(0, pairs // unroll, first_sums, 0)
        radius2 = positions[0] * positions[0] + positions[1] * positions[1]
        radius2 = radius2 + positions[2] * positions[2] + softening
        pull = -star_mass / (radius2 * jnp.sqrt(radius2))
        acceleration = []
        for k, value in enumerate(gains(0)):
            gain = lax.dot_general(
                first_hits, value, NN, precision=HIGHEST, preferred_element_type=jnp.float32
            )
            acceleration.append(gain + pull * positions[k] + react_out[me, k])
        for s, (_, arrival) in enumerate(react_copies):
            arrival.wait_recv()
            origin = lax.rem(me + work - (s + 1), work)
            for k in range(3):
                acceleration[k] = acceleration[k] + react_in[origin, k]
        for k in range(3):
            velocity = velocities[k] + time_step * acceleration[k]
            result[k] = positions[k] + time_step * velocity
            result[3 + k] = velocity
            result[6 + k] = acceleration[k]
        for copy in ghost_copies + [c for c, _ in sector_copies + rho_copies + react_copies]:
            copy.wait_send()
        return carry

    lax.fori_loop(0, STEPS, one_step, 0)
    for copy, _ in fixed_copies:
        copy.wait_send()


def unpack(result, new_pos, new_vel, acc_out, den_out):
    den_out[...] = result[9]
    for n, out in enumerate((new_pos, new_vel, acc_out)):
        for k in range(3):
            for t in range(den_out.shape[0]):
                out[k : k + 1, 128 * t : 128 * t + 128] = result[3 * n + k, t : t + 1, :]


def local(positions, velocities, masses, sound2, ghost_list, dens_list, pair_dest, pair_tiles):
    work, space = lax.axis_size("work"), lax.axis_size("space")
    particles = positions.shape[1]
    tiles = particles // 128
    pairs = pair_dest.shape[0]
    ghosts = ghost_list.shape[0]
    vmem = pl.BlockSpec(memory_space=pltpu.VMEM)
    f32 = jnp.float32
    i32 = jnp.int32
    packed = pl.pallas_call(
        functools.partial(kernel, work, space),
        out_shape=jax.ShapeDtypeStruct((10, tiles, 128), f32),
        in_specs=[pl.BlockSpec(memory_space=pltpu.HBM)] * 8,
        out_specs=vmem,
        scratch_shapes=[
            pltpu.VMEM((3, particles), f32),
            pltpu.VMEM((3, particles), f32),
            pltpu.VMEM((tiles, 128), f32),
            pltpu.VMEM((tiles, 128), f32),
            pltpu.SMEM((2, ghosts), i32),
            pltpu.SMEM(dens_list.shape, i32),
            pltpu.SMEM((1, pairs), i32),
            pltpu.SMEM((2, pairs), i32),
            pltpu.VMEM((1, pairs), i32),
            pltpu.VMEM((2, pairs), i32),
            pltpu.SemaphoreType.DMA((10,)),
            pltpu.VMEM((tiles, 7, 128, 128), f32),
            pltpu.VMEM((tiles, 2, 128, 128), f32),
            pltpu.VMEM((4, tiles + 2 * ghosts, 128), f32),
            pltpu.VMEM((pairs, 2, 128, 128), f32),
            pltpu.VMEM((tiles, 128, 128), f32),
            pltpu.VMEM((pairs, 2, 128, 128), jnp.bfloat16),
            pltpu.VMEM((8, pairs, 128), f32),
            pltpu.VMEM((2, 12 * pairs, 128), f32),
            pltpu.VMEM((2, 12 * pairs, 128), f32),
            pltpu.VMEM((work, 6, tiles, 128), f32),
            pltpu.VMEM((work, 2, tiles, 128), f32),
            pltpu.VMEM((work, 2, tiles, 128), f32),
            pltpu.VMEM((STEPS, 2, 4 * ghosts, 128), f32),
            pltpu.VMEM((STEPS, 2, 4 * ghosts, 128), f32),
            pltpu.VMEM((work, 3, tiles, 128), f32),
            pltpu.VMEM((work, 3, tiles, 128), f32),
            pltpu.SemaphoreType.DMA((4, work - 1)),
            pltpu.SemaphoreType.DMA((4, work - 1)),
            pltpu.SemaphoreType.DMA((STEPS, 2)),
            pltpu.SemaphoreType.DMA((STEPS, 2)),
        ],
        compiler_params=pltpu.CompilerParams(
            collective_id=0, has_side_effects=True, vmem_limit_bytes=63 * 1024 * 1024
        ),
        name="leapfrog",
    )(
        positions, velocities, masses.reshape(tiles, 128), sound2.reshape(tiles, 128),
        ghost_list.T, dens_list, pair_dest.T, pair_tiles.T,
    )
    wide = jax.ShapeDtypeStruct((3, particles), f32)
    outs = pl.pallas_call(
        unpack,
        out_shape=(wide, wide, wide, jax.ShapeDtypeStruct((tiles, 128), f32)),
        in_specs=[vmem],
        out_specs=(vmem,) * 4,
        name="unpack",
    )(packed)
    return outs[0], outs[1], outs[2], outs[3].reshape(particles)


def solution(mesh):
    return jax.shard_map(
        local,
        mesh=mesh,
        in_specs=(
            P(None, ("space", "work")),
            P(None, ("space", "work")),
            P(("space", "work")),
            P(("space", "work")),
            P(("space", "work"), None),
            P(("space", "work"), None),
            P(("space", "work"), None),
            P(("space", "work"), None),
        ),
        out_specs=(
            P(None, ("space", "work")),
            P(None, ("space", "work")),
            P(None, ("space", "work")),
            P(("space", "work")),
        ),
        check_vma=False,
    )
```

```python
import functools
import math

import jax
import jax.numpy as jnp
from jax import lax
from jax.experimental import pallas as pl
from jax.experimental.pallas import tpu as pltpu
from jax.sharding import PartitionSpec as P

STEPS = 2
MESH = pl.DeviceIdType.MESH
NT = (((1,), (1,)), ((), ()))
NN = (((1,), (0,)), ((), ()))
LOG2E = math.log2(math.e)
ROOT_LOG2E = math.sqrt(LOG2E)

star_mass = 0.5
softening = 0.1
time_step = 0.1


def inverse(value):
    guess = pl.reciprocal(value, approx=True)
    return guess * (2.0 - value * guess)


def halves(value):
    high = value.astype(jnp.bfloat16)
    return high, (value - high.astype(jnp.float32)).astype(jnp.bfloat16)


def kernel(
    work, space,
    pos_in, vel_in, mass_in, snd_in, ghost_in, dens_in, dest_in, tiles_in,
    result,
    pos, vel, mass, snd, ghost, dens, dest_s, tiles_s, dest_v, tiles_v, load_sem,
    spread, spread_rho, cand, factors, totals, weights, gathered, moments, sums,
    sector, fixed, rho, ghosts_out, ghosts_in, react_out, react_in,
    send_sem, recv_sem, ghost_send, ghost_recv,
):
    tiles = mass.shape[0]
    pairs = dest_v.shape[1]
    ghost_count = ghost.shape[1]
    listed = dens.shape[1]
    unroll = math.gcd(pairs, 4)
    loads = []
    for n, (source, target) in enumerate((
        (pos_in, pos), (vel_in, vel), (mass_in, mass), (snd_in, snd), (ghost_in, ghost),
        (dens_in, dens), (dest_in, dest_s), (tiles_in, tiles_s), (dest_in, dest_v),
        (tiles_in, tiles_v),
    )):
        copy = pltpu.make_async_copy(source, target, load_sem.at[n])
        copy.start()
        loads.append(copy)
    me = lax.axis_index("work")
    here = lax.axis_index("space")
    above, below = lax.rem(here + 1, space), lax.rem(here + space - 1, space)

    barrier = pltpu.get_barrier_semaphore()
    for s in range(1, work):
        pl.semaphore_signal(
            barrier, inc=1, device_id={"work": lax.rem(me + s, work)}, device_id_type=MESH
        )
    for z in (above, below):
        pl.semaphore_signal(barrier, inc=1, device_id={"space": z}, device_id_type=MESH)

    def everyone(kind, source, target, own_slot):
        copies = []
        for s in range(1, work):
            to, origin = lax.rem(me + s, work), lax.rem(me + work - s, work)
            if own_slot:
                out, into, arriving = source.at[me], target.at[me], target.at[origin]
            else:
                out, into, arriving = source.at[to], target.at[me], target.at[origin]
            sems = (send_sem.at[kind, s - 1], recv_sem.at[kind, s - 1])
            copy = pltpu.make_async_remote_copy(
                src_ref=out, dst_ref=into, send_sem=sems[0], recv_sem=sems[1],
                device_id={"work": to}, device_id_type=MESH,
            )
            arrival = pltpu.make_async_remote_copy(
                src_ref=arriving, dst_ref=arriving, send_sem=sems[0], recv_sem=sems[1],
                device_id={"work": to}, device_id_type=MESH,
            )
            copies.append((copy, arrival))
        return copies

    for copy in loads:
        copy.wait()
    masses = mass[...]
    sound2 = snd[...]
    sound = jnp.sqrt(sound2)
    for k in range(3):
        for t in range(tiles):
            result[k, t : t + 1, :] = pos[k : k + 1, 128 * t : 128 * t + 128]
            result[3 + k, t : t + 1, :] = vel[k : k + 1, 128 * t : 128 * t + 128]
    fixed[me, 0] = masses
    fixed[me, 1] = sound
    cand[3, 0:tiles, :] = jnp.log2(masses)
    lanes = lax.broadcasted_iota(jnp.int32, (128, 128), 1)
    owner_hits = (
        lax.broadcasted_iota(jnp.int32, (work * tiles, pairs), 0)
        == dest_v[...] * tiles + tiles_v[1:2, :]
    ).astype(jnp.float32).astype(jnp.bfloat16)
    first_hits = (
        lax.broadcasted_iota(jnp.int32, (tiles, pairs), 0) == tiles_v[0:1, :]
    ).astype(jnp.float32).astype(jnp.bfloat16)

    fixed_copies = everyone(3, fixed, fixed, True)

    def one_step(step, carry):
        positions = [result[k] for k in range(3)]
        velocities = [result[3 + k] for k in range(3)]
        for k in range(3):
            cand[k, 0:tiles, :] = positions[k] * ROOT_LOG2E
            sector[me, k] = positions[k]
            sector[me, 3 + k] = velocities[k]
        for way in range(2):
            rows = [
                cand[k, pl.ds(ghost[way, j], 1), :] for k in range(4) for j in range(ghost_count)
            ]
            ghosts_out[step, way] = jnp.concatenate(rows, axis=0)

        @pl.when(step == 0)
        def _():
            pl.semaphore_wait(barrier, work + 1)

        ghost_copies = []
        for way, z in enumerate((above, below)):
            copy = pltpu.make_async_remote_copy(
                src_ref=ghosts_out.at[step, way], dst_ref=ghosts_in.at[step, way],
                send_sem=ghost_send.at[step, way], recv_sem=ghost_recv.at[step, way],
                device_id={"space": z}, device_id_type=MESH,
            )
            copy.start()
            ghost_copies.append(copy)
        sector_copies = everyone(0, sector, sector, True)
        for copy, _ in sector_copies:
            copy.start()

        @pl.when(step == 0)
        def _():
            for copy, _ in fixed_copies:
                copy.start()

        def gap2(home, row):
            gaps = [home[k] - row[k] for k in range(3)]
            return gaps[0] * gaps[0] + gaps[1] * gaps[1] + gaps[2] * gaps[2]

        def wide_row(number):
            return [
                jnp.broadcast_to(cand[k, pl.ds(number, 1), :], (32, 128)) for k in range(4)
            ]

        planes = positions + velocities + [sound]
        blank = jnp.zeros((128 - tiles * len(planes), 128), jnp.float32)
        columns = jnp.concatenate(planes + [blank], axis=0).T

        def spread_tile(t, carry):
            turned = pltpu.roll(columns, lax.rem(128 - t, 128), 1)
            for q in range(len(planes)):
                spread[t, q] = jnp.broadcast_to(
                    turned[:, q * tiles : q * tiles + 1], (128, 128)
                )
            return carry

        def own_density(t, carry):
            row = [jnp.broadcast_to(cand[k, pl.ds(t, 1), :], (128, 128)) for k in range(4)]
            home = [spread[t, k] * ROOT_LOG2E for k in range(3)]
            totals[t] = jnp.exp2(row[3] - gap2(home, row))
            return carry

        lax.fori_loop(0, tiles, spread_tile, 0)
        lax.fori_loop(0, tiles, own_density, 0)
        for copy in ghost_copies:
            copy.wait_recv()
        for way in range(2):
            first = tiles + way * ghost_count
            for k in range(4):
                cand[k, first : first + ghost_count, :] = ghosts_in[
                    step, way, k * ghost_count : (k + 1) * ghost_count, :
                ]

        def density_of(first, carry):
            for t in [first * 2, first * 2 + 1]:
                rows = [wide_row(dens[t, c]) for c in range(listed)]
                parts = []
                for i in range(0, 128, 32):
                    home = [spread[t, k, i : i + 32, :] * ROOT_LOG2E for k in range(3)]
                    part = totals[t, i : i + 32, :]
                    for row in rows:
                        part = part + jnp.exp2(row[3] - gap2(home, row))
                    parts.append(jnp.sum(part, axis=1, keepdims=True))
                spread_rho[t, 0] = jnp.broadcast_to(jnp.concatenate(parts, axis=0), (128, 128))
            return carry

        lax.fori_loop(0, tiles // 2, density_of, 0)
        columns = jnp.zeros((128, 128), jnp.float32)
        for t in range(tiles):
            columns = jnp.where(lanes == t, spread_rho[t, 0], columns)
        density = columns.T[0:tiles, :]
        result[9] = density
        rho[me, 0] = density
        rho[me, 1] = sound2 / density
        rho_copies = everyone(1, rho, rho, True)
        for copy, _ in rho_copies:
            copy.start()

        def spread_pressure(t, carry):
            speed = spread[t, 6]
            spread_rho[t, 1] = speed * speed * inverse(spread_rho[t, 0])
            return carry

        lax.fori_loop(0, tiles, spread_pressure, 0)

        for _, arrival in sector_copies:
            arrival.wait_recv()

        @pl.when(step == 0)
        def _():
            for _, arrival in fixed_copies:
                arrival.wait_recv()

        def pair_factors(turn, carry):
            for u in range(unroll):
                p = turn * unroll + u
                a, owner, b = tiles_s[0, p], dest_s[0, p], tiles_s[1, p]
                row = [sector[owner, k, pl.ds(b, 1), :] for k in range(6)]
                row.append(fixed[owner, 1, pl.ds(b, 1), :])
                kept = [sector[me, k, pl.ds(a, 1), :] for k in range(3)]
                kept.append(fixed[me, 0, pl.ds(a, 1), :])
                kept = kept + row[0:3] + [fixed[owner, 0, pl.ds(b, 1), :]]
                row = [jnp.broadcast_to(value, (64, 128)) for value in row]
                results = []
                for i in range(0, 128, 64):
                    home = [spread[a, k, i : i + 64, :] for k in range(7)]
                    gaps = [home[k] - row[k] for k in range(3)]
                    distance2 = gaps[0] * gaps[0] + gaps[1] * gaps[1] + gaps[2] * gaps[2]
                    approach = (home[3] - row[3]) * gaps[0]
                    approach = approach + (home[4] - row[4]) * gaps[1]
                    approach = approach + (home[5] - row[5]) * gaps[2]
                    closing = jnp.minimum(approach * inverse(distance2 + 0.01), 0.0)
                    twice = jnp.exp2(1.0 - distance2 * LOG2E)
                    results.append(
                        (i, twice, twice * closing * (4.0 * closing - (home[6] + row[6])))
                    )
                for i, twice, viscous in results:
                    factors[p, 0, i : i + 64, :] = twice
                    factors[p, 1, i : i + 64, :] = viscous
                for k in range(8):
                    gathered[k, pl.ds(p, 1), :] = kept[k]
            return carry

        lax.fori_loop(0, pairs // unroll, pair_factors, 0)
        for side in range(2):
            mass_rows = gathered[4 * side + 3]
            for k in range(4):
                value = mass_rows if k == 3 else mass_rows * gathered[4 * side + k]
                for g in range(3):
                    piece = value.astype(jnp.bfloat16).astype(jnp.float32)
                    value = value - piece
                    moments[side, pl.ds((4 * g + k) * pairs, pairs), :] = piece
        for _, arrival in rho_copies:
            arrival.wait_recv()

        def own_moments(side, p):
            rows = moments[side, pl.ds(p, 12, stride=pairs), :].astype(jnp.bfloat16)
            return jnp.concatenate([rows, rows], axis=1)

        def gains(side):
            moved = [
                sums[side, pl.ds(k * pairs, pairs), :]
                + sums[side, pl.ds((4 + k) * pairs, pairs), :]
                + sums[side, pl.ds((8 + k) * pairs, pairs), :]
                for k in range(4)
            ]
            return [gathered[4 * side + k] * moved[3] - moved[k] for k in range(3)]

        def pair_weights(turn, carry):
            results = []
            for u in range(unroll):
                p = turn * unroll + u
                a, owner, b = tiles_s[0, p], dest_s[0, p], tiles_s[1, p]
                row_rho = jnp.broadcast_to(rho[owner, 0, pl.ds(b, 1), :], (128, 128))
                row_pressure = jnp.broadcast_to(rho[owner, 1, pl.ds(b, 1), :], (128, 128))
                weight = factors[p, 0] * (spread_rho[a, 1] + row_pressure)
                weight = weight + factors[p, 1] * inverse(spread_rho[a, 0] + row_rho)
                high, low = halves(weight)
                moved = lax.dot_general(
                    own_moments(0, p), jnp.concatenate([high, low], axis=0),
                    NN, preferred_element_type=jnp.float32,
                )
                results.append((p, high, low, moved))
            for p, high, low, moved in results:
                weights[p, 0] = high
                weights[p, 1] = low
                sums[1, pl.ds(p, 12, stride=pairs), :] = moved
            return carry

        def first_sums(turn, carry):
            results = []
            for u in range(unroll):
                p = turn * unroll + u
                results.append((p, lax.dot_general(
                    own_moments(1, p),
                    jnp.concatenate([weights[p, 0], weights[p, 1]], axis=1),
                    NT, preferred_element_type=jnp.float32,
                )))
            for p, moved in results:
                sums[0, pl.ds(p, 12, stride=pairs), :] = moved
            return carry

        lax.fori_loop(0, pairs // unroll, pair_weights, 0)
        reaction = added(owner_hits, gains(1))
        for k in range(3):
            for w in range(work):
                react_out[w, k] = reaction[w * tiles : (w + 1) * tiles, 128 * k : 128 * k + 128]
        react_copies = everyone(2, react_out, react_in, False)
        for copy, _ in react_copies:
            copy.start()
        lax.fori_loop(0, pairs // unroll, first_sums, 0)
        radius2 = positions[0] * positions[0] + positions[1] * positions[1]
        radius2 = radius2 + positions[2] * positions[2] + softening
        pull = -star_mass / (radius2 * jnp.sqrt(radius2))
        acceleration = []
        gain = added(first_hits, gains(0))
        for k in range(3):
            own = gain[:, 128 * k : 128 * k + 128]
            acceleration.append(own + pull * positions[k] + react_out[me, k])
        for s, (_, arrival) in enumerate(react_copies):
            arrival.wait_recv()
            origin = lax.rem(me + work - (s + 1), work)
            for k in range(3):
                acceleration[k] = acceleration[k] + react_in[origin, k]
        for k in range(3):
            velocity = velocities[k] + time_step * acceleration[k]
            result[k] = positions[k] + time_step * velocity
            result[3 + k] = velocity
            result[6 + k] = acceleration[k]
        for copy in ghost_copies + [c for c, _ in sector_copies + rho_copies + react_copies]:
            copy.wait_send()
        return carry

    lax.fori_loop(0, STEPS, one_step, 0)
    for copy, _ in fixed_copies:
        copy.wait_send()


def added(hits, values):
    value = jnp.concatenate(values, axis=1)
    pieces = []
    for _ in range(3):
        piece = value.astype(jnp.bfloat16)
        value = value - piece.astype(jnp.float32)
        pieces.append(piece)
    return lax.dot_general(
        jnp.concatenate([hits] * 3, axis=1), jnp.concatenate(pieces, axis=0), NN,
        preferred_element_type=jnp.float32,
    )


def unpack(result, new_pos, new_vel, acc_out, den_out):
    den_out[...] = result[9]
    for n, out in enumerate((new_pos, new_vel, acc_out)):
        for k in range(3):
            for t in range(den_out.shape[0]):
                out[k : k + 1, 128 * t : 128 * t + 128] = result[3 * n + k, t : t + 1, :]


def local(positions, velocities, masses, sound2, ghost_list, dens_list, pair_dest, pair_tiles):
    work, space = lax.axis_size("work"), lax.axis_size("space")
    particles = positions.shape[1]
    tiles = particles // 128
    pairs = pair_dest.shape[0]
    ghosts = ghost_list.shape[0]
    vmem = pl.BlockSpec(memory_space=pltpu.VMEM)
    f32 = jnp.float32
    i32 = jnp.int32
    packed = pl.pallas_call(
        functools.partial(kernel, work, space),
        out_shape=jax.ShapeDtypeStruct((10, tiles, 128), f32),
        in_specs=[pl.BlockSpec(memory_space=pltpu.HBM)] * 8,
        out_specs=vmem,
        scratch_shapes=[
            pltpu.VMEM((3, particles), f32),
            pltpu.VMEM((3, particles), f32),
            pltpu.VMEM((tiles, 128), f32),
            pltpu.VMEM((tiles, 128), f32),
            pltpu.SMEM((2, ghosts), i32),
            pltpu.SMEM(dens_list.shape, i32),
            pltpu.SMEM((1, pairs), i32),
            pltpu.SMEM((2, pairs), i32),
            pltpu.VMEM((1, pairs), i32),
            pltpu.VMEM((2, pairs), i32),
            pltpu.SemaphoreType.DMA((10,)),
            pltpu.VMEM((tiles, 7, 128, 128), f32),
            pltpu.VMEM((tiles, 2, 128, 128), f32),
            pltpu.VMEM((4, tiles + 2 * ghosts, 128), f32),
            pltpu.VMEM((pairs, 2, 128, 128), f32),
            pltpu.VMEM((tiles, 128, 128), f32),
            pltpu.VMEM((pairs, 2, 128, 128), jnp.bfloat16),
            pltpu.VMEM((8, pairs, 128), f32),
            pltpu.VMEM((2, 12 * pairs, 128), f32),
            pltpu.VMEM((2, 12 * pairs, 128), f32),
            pltpu.VMEM((work, 6, tiles, 128), f32),
            pltpu.VMEM((work, 2, tiles, 128), f32),
            pltpu.VMEM((work, 2, tiles, 128), f32),
            pltpu.VMEM((STEPS, 2, 4 * ghosts, 128), f32),
            pltpu.VMEM((STEPS, 2, 4 * ghosts, 128), f32),
            pltpu.VMEM((work, 3, tiles, 128), f32),
            pltpu.VMEM((work, 3, tiles, 128), f32),
            pltpu.SemaphoreType.DMA((4, work - 1)),
            pltpu.SemaphoreType.DMA((4, work - 1)),
            pltpu.SemaphoreType.DMA((STEPS, 2)),
            pltpu.SemaphoreType.DMA((STEPS, 2)),
        ],
        compiler_params=pltpu.CompilerParams(
            collective_id=0, has_side_effects=True, vmem_limit_bytes=63 * 1024 * 1024
        ),
        name="leapfrog",
    )(
        positions, velocities, masses.reshape(tiles, 128), sound2.reshape(tiles, 128),
        ghost_list.T, dens_list, pair_dest.T, pair_tiles.T,
    )
    wide = jax.ShapeDtypeStruct((3, particles), f32)
    outs = pl.pallas_call(
        unpack,
        out_shape=(wide, wide, wide, jax.ShapeDtypeStruct((tiles, 128), f32)),
        in_specs=[vmem],
        out_specs=(vmem,) * 4,
        name="unpack",
    )(packed)
    return outs[0], outs[1], outs[2], outs[3].reshape(particles)


def solution(mesh):
    return jax.shard_map(
        local,
        mesh=mesh,
        in_specs=(
            P(None, ("space", "work")),
            P(None, ("space", "work")),
            P(("space", "work")),
            P(("space", "work")),
            P(("space", "work"), None),
            P(("space", "work"), None),
            P(("space", "work"), None),
            P(("space", "work"), None),
        ),
        out_specs=(
            P(None, ("space", "work")),
            P(None, ("space", "work")),
            P(None, ("space", "work")),
            P(("space", "work")),
        ),
        check_vma=False,
    )
```

```python
import functools
import math

import jax
import jax.numpy as jnp
from jax import lax
from jax.experimental import pallas as pl
from jax.experimental.pallas import tpu as pltpu
from jax.sharding import PartitionSpec as P

STEPS = 2
MESH = pl.DeviceIdType.MESH
NT = (((1,), (1,)), ((), ()))
NN = (((1,), (0,)), ((), ()))
LOG2E = math.log2(math.e)
ROOT_LOG2E = math.sqrt(LOG2E)

star_mass = 0.5
softening = 0.1
time_step = 0.1


def inverse(value):
    guess = pl.reciprocal(value, approx=True)
    return guess * (2.0 - value * guess)


def halves(value):
    high = value.astype(jnp.bfloat16)
    return high, (value - high.astype(jnp.float32)).astype(jnp.bfloat16)


def kernel(
    work, space,
    pos_in, vel_in, mass_in, snd_in, ghost_in, dens_in, dest_in, tiles_in,
    result,
    pos, vel, mass, snd, ghost, dens, dest_s, tiles_s, dest_v, tiles_v, load_sem,
    spread, spread_rho, cand, factors, totals, weights, gathered, moments, sums,
    sector, fixed, rho, pressure, ghosts_out, ghosts_in, react_out, react_in,
    send_sem, recv_sem, ghost_send, ghost_recv,
):
    tiles = mass.shape[0]
    pairs = dest_v.shape[1]
    ghost_count = ghost.shape[1]
    listed = dens.shape[1]
    unroll, tile_unroll = math.gcd(pairs, 8), math.gcd(tiles, 4)
    loads = []
    for n, (source, target) in enumerate((
        (pos_in, pos), (vel_in, vel), (mass_in, mass), (snd_in, snd), (ghost_in, ghost),
        (dens_in, dens), (dest_in, dest_s), (tiles_in, tiles_s), (dest_in, dest_v),
        (tiles_in, tiles_v),
    )):
        copy = pltpu.make_async_copy(source, target, load_sem.at[n])
        copy.start()
        loads.append(copy)
    me = lax.axis_index("work")
    here = lax.axis_index("space")
    above, below = lax.rem(here + 1, space), lax.rem(here + space - 1, space)

    partners = []
    for s in reversed(range(1, work)):
        partner, digit = 0, 1
        while digit < work:
            partner = partner + digit * (((me // digit) + (s // digit)) % 2)
            digit = 2 * digit
        partners.append(partner)

    barrier = pltpu.get_barrier_semaphore()
    for partner in partners:
        pl.semaphore_signal(barrier, inc=1, device_id={"work": partner}, device_id_type=MESH)
    for z in (above, below):
        pl.semaphore_signal(barrier, inc=1, device_id={"space": z}, device_id_type=MESH)

    def everyone(kind, source, target, own_slot):
        copies = []
        for s, partner in enumerate(partners):
            out = source.at[me] if own_slot else source.at[partner]
            into, arriving = target.at[me], target.at[partner]
            sems = (send_sem.at[kind, s], recv_sem.at[kind, s])
            copy = pltpu.make_async_remote_copy(
                src_ref=out, dst_ref=into, send_sem=sems[0], recv_sem=sems[1],
                device_id={"work": partner}, device_id_type=MESH,
            )
            arrival = pltpu.make_async_remote_copy(
                src_ref=arriving, dst_ref=arriving, send_sem=sems[0], recv_sem=sems[1],
                device_id={"work": partner}, device_id_type=MESH,
            )
            copies.append((copy, arrival))
        return copies

    for copy in loads:
        copy.wait()
    masses = mass[...]
    sound2 = snd[...]
    sound = jnp.sqrt(sound2)
    for k in range(3):
        for t in range(tiles):
            result[k, t : t + 1, :] = pos[k : k + 1, 128 * t : 128 * t + 128]
            result[3 + k, t : t + 1, :] = vel[k : k + 1, 128 * t : 128 * t + 128]
    fixed[me, 0] = masses
    fixed[me, 1] = sound
    cand[3, 0:tiles, :] = jnp.log2(masses)
    lanes = lax.broadcasted_iota(jnp.int32, (128, 128), 1)
    owner_hits = (
        lax.broadcasted_iota(jnp.int32, (work * tiles, pairs), 0)
        == dest_v[...] * tiles + tiles_v[1:2, :]
    ).astype(jnp.float32).astype(jnp.bfloat16)
    first_hits = (
        lax.broadcasted_iota(jnp.int32, (tiles, pairs), 0) == tiles_v[0:1, :]
    ).astype(jnp.float32).astype(jnp.bfloat16)

    fixed_copies = everyone(3, fixed, fixed, True)

    def one_step(step, carry):
        positions = [result[k] for k in range(3)]
        velocities = [result[3 + k] for k in range(3)]
        for k in range(3):
            cand[k, 0:tiles, :] = positions[k] * ROOT_LOG2E
            sector[me, k] = positions[k]
            sector[me, 3 + k] = velocities[k]
        for way in range(2):
            rows = [
                cand[k, pl.ds(ghost[way, j], 1), :] for k in range(4) for j in range(ghost_count)
            ]
            ghosts_out[step, way] = jnp.concatenate(rows, axis=0)

        @pl.when(step == 0)
        def _():
            pl.semaphore_wait(barrier, work + 1)

        ghost_copies = []
        for way, z in enumerate((above, below)):
            copy = pltpu.make_async_remote_copy(
                src_ref=ghosts_out.at[step, way], dst_ref=ghosts_in.at[step, way],
                send_sem=ghost_send.at[step, way], recv_sem=ghost_recv.at[step, way],
                device_id={"space": z}, device_id_type=MESH,
            )
            copy.start()
            ghost_copies.append(copy)
        sector_copies = everyone(0, sector, sector, True)
        for copy, _ in sector_copies:
            copy.start()

        @pl.when(step == 0)
        def _():
            for copy, _ in fixed_copies:
                copy.start()

        def gap2(home, row):
            gaps = [home[k] - row[k] for k in range(3)]
            return gaps[0] * gaps[0] + gaps[1] * gaps[1] + gaps[2] * gaps[2]

        def wide_row(number):
            return [
                jnp.broadcast_to(cand[k, pl.ds(number, 1), :], (32, 128)) for k in range(4)
            ]

        planes = positions + velocities + [sound]
        blank = jnp.zeros((128 - tiles * len(planes), 128), jnp.float32)
        columns = jnp.concatenate(planes + [blank], axis=0).T

        for t in range(tiles):
            for q in range(len(planes)):
                c = q * tiles + t
                spread[t, q] = jnp.broadcast_to(columns[:, c : c + 1], (128, 128))
        for t in range(tiles):
            row = [jnp.broadcast_to(cand[k, t : t + 1, :], (32, 128)) for k in range(4)]
            for i in range(0, 128, 32):
                home = [spread[t, k, i : i + 32, :] * ROOT_LOG2E for k in range(3)]
                totals[t, i : i + 32, :] = jnp.exp2(row[3] - gap2(home, row))
        for copy in ghost_copies:
            copy.wait_recv()
        for way in range(2):
            first = tiles + way * ghost_count
            for k in range(4):
                cand[k, first : first + ghost_count, :] = ghosts_in[
                    step, way, k * ghost_count : (k + 1) * ghost_count, :
                ]

        def density_of(first, carry):
            for t in [first * tile_unroll + u for u in range(tile_unroll)]:
                rows = [wide_row(dens[t, c]) for c in range(listed)]
                parts = []
                for i in range(0, 128, 32):
                    home = [spread[t, k, i : i + 32, :] * ROOT_LOG2E for k in range(3)]
                    part = totals[t, i : i + 32, :]
                    for row in rows:
                        part = part + jnp.exp2(row[3] - gap2(home, row))
                    parts.append(jnp.sum(part, axis=1, keepdims=True))
                spread_rho[t, 0] = jnp.broadcast_to(jnp.concatenate(parts, axis=0), (128, 128))
            return carry

        lax.fori_loop(0, tiles // tile_unroll, density_of, 0)
        columns = jnp.zeros((128, 128), jnp.float32)
        for t in range(tiles):
            columns = jnp.where(lanes == t, spread_rho[t, 0], columns)
        density = columns.T[0:tiles, :]
        result[9] = density
        rho[me] = density
        rho_copies = everyone(1, rho, rho, True)
        for copy, _ in rho_copies:
            copy.start()

        for t in range(tiles):
            speed = spread[t, 6]
            spread_rho[t, 1] = speed * speed * inverse(spread_rho[t, 0])

        for _, arrival in sector_copies:
            arrival.wait_recv()

        @pl.when(step == 0)
        def _():
            for _, arrival in fixed_copies:
                arrival.wait_recv()

        def pair_factors(turn, carry):
            for u in range(unroll):
                p = turn * unroll + u
                a, owner, b = tiles_s[0, p], dest_s[0, p], tiles_s[1, p]
                row = [sector[owner, k, pl.ds(b, 1), :] for k in range(6)]
                row.append(fixed[owner, 1, pl.ds(b, 1), :])
                kept = [sector[me, k, pl.ds(a, 1), :] for k in range(3)]
                kept.append(fixed[me, 0, pl.ds(a, 1), :])
                kept = kept + row[0:3] + [fixed[owner, 0, pl.ds(b, 1), :]]
                row = [jnp.broadcast_to(value, (32, 128)) for value in row]
                for i in range(0, 128, 32):
                    home = [spread[a, k, i : i + 32, :] for k in range(7)]
                    gaps = [home[k] - row[k] for k in range(3)]
                    distance2 = gaps[0] * gaps[0] + gaps[1] * gaps[1] + gaps[2] * gaps[2]
                    approach = (home[3] - row[3]) * gaps[0]
                    approach = approach + (home[4] - row[4]) * gaps[1]
                    approach = approach + (home[5] - row[5]) * gaps[2]
                    closing = jnp.minimum(approach * inverse(distance2 + 0.01), 0.0)
                    twice = jnp.exp2(1.0 - distance2 * LOG2E)
                    factors[p, 0, i : i + 32, :] = twice
                    factors[p, 1, i : i + 32, :] = (
                        twice * closing * (4.0 * closing - (home[6] + row[6]))
                    )
                for k in range(8):
                    gathered[k, pl.ds(p, 1), :] = kept[k]
            return carry

        lax.fori_loop(0, pairs // unroll, pair_factors, 0)
        for side in range(2):
            mass_rows = gathered[4 * side + 3]
            for k in range(4):
                value = mass_rows if k == 3 else mass_rows * gathered[4 * side + k]
                for g in range(3):
                    piece = value.astype(jnp.bfloat16).astype(jnp.float32)
                    value = value - piece
                    moments[side, pl.ds((4 * g + k) * pairs, pairs), :] = piece
        for _, arrival in rho_copies:
            arrival.wait_recv()
        for w in range(work):
            pressure[w] = fixed[w, 1] * fixed[w, 1] / rho[w]

        def own_moments(side, p):
            rows = moments[side, pl.ds(p, 12, stride=pairs), :].astype(jnp.bfloat16)
            return jnp.concatenate([rows, rows], axis=1)

        def gains(side):
            moved = [
                sums[side, pl.ds(k * pairs, pairs), :]
                + sums[side, pl.ds((4 + k) * pairs, pairs), :]
                + sums[side, pl.ds((8 + k) * pairs, pairs), :]
                for k in range(4)
            ]
            return [gathered[4 * side + k] * moved[3] - moved[k] for k in range(3)]

        def pair_weights(turn, carry):
            results = []
            for u in range(unroll):
                p = turn * unroll + u
                a, owner, b = tiles_s[0, p], dest_s[0, p], tiles_s[1, p]
                row_rho = jnp.broadcast_to(rho[owner, pl.ds(b, 1), :], (32, 128))
                row_pressure = jnp.broadcast_to(pressure[owner, pl.ds(b, 1), :], (32, 128))
                parts = []
                for i in range(0, 128, 32):
                    own = pl.ds(i, 32)
                    weight = factors[p, 0, own, :] * (spread_rho[a, 1, own, :] + row_pressure)
                    weight = weight + factors[p, 1, own, :] * inverse(
                        spread_rho[a, 0, own, :] + row_rho
                    )
                    high, low = halves(weight)
                    weights[p, 0, own, :] = high
                    weights[p, 1, own, :] = low
                    parts.append((high, low))
                stacked = jnp.concatenate([h for h, _ in parts] + [l for _, l in parts], axis=0)
                results.append((p, lax.dot_general(
                    own_moments(0, p), stacked, NN, preferred_element_type=jnp.float32
                )))
            for p, moved in results:
                sums[1, pl.ds(p, 12, stride=pairs), :] = moved
            return carry

        def first_sums(turn, carry):
            results = []
            for u in range(unroll):
                p = turn * unroll + u
                results.append((p, lax.dot_general(
                    own_moments(1, p),
                    jnp.concatenate([weights[p, 0], weights[p, 1]], axis=1),
                    NT, preferred_element_type=jnp.float32,
                )))
            for p, moved in results:
                sums[0, pl.ds(p, 12, stride=pairs), :] = moved
            return carry

        lax.fori_loop(0, pairs // unroll, pair_weights, 0)
        reaction = added(owner_hits, gains(1))
        for k in range(3):
            for w in range(work):
                react_out[w, k] = reaction[w * tiles : (w + 1) * tiles, 128 * k : 128 * k + 128]
        react_copies = everyone(2, react_out, react_in, False)
        for copy, _ in react_copies:
            copy.start()
        lax.fori_loop(0, pairs // unroll, first_sums, 0)
        radius2 = positions[0] * positions[0] + positions[1] * positions[1]
        radius2 = radius2 + positions[2] * positions[2] + softening
        pull = -star_mass / (radius2 * jnp.sqrt(radius2))
        acceleration = []
        gain = added(first_hits, gains(0))
        for k in range(3):
            own = gain[:, 128 * k : 128 * k + 128]
            acceleration.append(own + pull * positions[k] + react_out[me, k])
        for partner, (_, arrival) in zip(partners, react_copies):
            arrival.wait_recv()
            for k in range(3):
                acceleration[k] = acceleration[k] + react_in[partner, k]
        for k in range(3):
            velocity = velocities[k] + time_step * acceleration[k]
            result[k] = positions[k] + time_step * velocity
            result[3 + k] = velocity
            result[6 + k] = acceleration[k]
        for copy in ghost_copies + [c for c, _ in sector_copies + rho_copies + react_copies]:
            copy.wait_send()
        return carry

    lax.fori_loop(0, STEPS, one_step, 0)
    for copy, _ in fixed_copies:
        copy.wait_send()


def added(hits, values):
    value = jnp.concatenate(values, axis=1)
    pieces = []
    for _ in range(3):
        piece = value.astype(jnp.bfloat16)
        value = value - piece.astype(jnp.float32)
        pieces.append(piece)
    return lax.dot_general(
        jnp.concatenate([hits] * 3, axis=1), jnp.concatenate(pieces, axis=0), NN,
        preferred_element_type=jnp.float32,
    )


def unpack(result, new_pos, new_vel, acc_out, den_out):
    den_out[...] = result[9]
    for n, out in enumerate((new_pos, new_vel, acc_out)):
        for k in range(3):
            for t in range(den_out.shape[0]):
                out[k : k + 1, 128 * t : 128 * t + 128] = result[3 * n + k, t : t + 1, :]


def local(positions, velocities, masses, sound2, ghost_list, dens_list, pair_dest, pair_tiles):
    work, space = lax.axis_size("work"), lax.axis_size("space")
    particles = positions.shape[1]
    tiles = particles // 128
    pairs = pair_dest.shape[0]
    ghosts = ghost_list.shape[0]
    vmem = pl.BlockSpec(memory_space=pltpu.VMEM)
    f32 = jnp.float32
    i32 = jnp.int32
    packed = pl.pallas_call(
        functools.partial(kernel, work, space),
        out_shape=jax.ShapeDtypeStruct((10, tiles, 128), f32),
        in_specs=[pl.BlockSpec(memory_space=pltpu.HBM)] * 8,
        out_specs=vmem,
        scratch_shapes=[
            pltpu.VMEM((3, particles), f32),
            pltpu.VMEM((3, particles), f32),
            pltpu.VMEM((tiles, 128), f32),
            pltpu.VMEM((tiles, 128), f32),
            pltpu.SMEM((2, ghosts), i32),
            pltpu.SMEM(dens_list.shape, i32),
            pltpu.SMEM((1, pairs), i32),
            pltpu.SMEM((2, pairs), i32),
            pltpu.VMEM((1, pairs), i32),
            pltpu.VMEM((2, pairs), i32),
            pltpu.SemaphoreType.DMA((10,)),
            pltpu.VMEM((tiles, 7, 128, 128), f32),
            pltpu.VMEM((tiles, 2, 128, 128), f32),
            pltpu.VMEM((4, tiles + 2 * ghosts, 128), f32),
            pltpu.VMEM((pairs, 2, 128, 128), f32),
            pltpu.VMEM((tiles, 128, 128), f32),
            pltpu.VMEM((pairs, 2, 128, 128), jnp.bfloat16),
            pltpu.VMEM((8, pairs, 128), f32),
            pltpu.VMEM((2, 12 * pairs, 128), f32),
            pltpu.VMEM((2, 12 * pairs, 128), f32),
            pltpu.VMEM((work, 6, tiles, 128), f32),
            pltpu.VMEM((work, 2, tiles, 128), f32),
            pltpu.VMEM((work, tiles, 128), f32),
            pltpu.VMEM((work, tiles, 128), f32),
            pltpu.VMEM((STEPS, 2, 4 * ghosts, 128), f32),
            pltpu.VMEM((STEPS, 2, 4 * ghosts, 128), f32),
            pltpu.VMEM((work, 3, tiles, 128), f32),
            pltpu.VMEM((work, 3, tiles, 128), f32),
            pltpu.SemaphoreType.DMA((4, work - 1)),
            pltpu.SemaphoreType.DMA((4, work - 1)),
            pltpu.SemaphoreType.DMA((STEPS, 2)),
            pltpu.SemaphoreType.DMA((STEPS, 2)),
        ],
        compiler_params=pltpu.CompilerParams(
            collective_id=0, has_side_effects=True, vmem_limit_bytes=63 * 1024 * 1024
        ),
        name="leapfrog",
    )(
        positions, velocities, masses.reshape(tiles, 128), sound2.reshape(tiles, 128),
        ghost_list.T, dens_list, pair_dest.T, pair_tiles.T,
    )
    wide = jax.ShapeDtypeStruct((3, particles), f32)
    outs = pl.pallas_call(
        unpack,
        out_shape=(wide, wide, wide, jax.ShapeDtypeStruct((tiles, 128), f32)),
        in_specs=[vmem],
        out_specs=(vmem,) * 4,
        name="unpack",
    )(packed)
    return outs[0], outs[1], outs[2], outs[3].reshape(particles)


def solution(mesh):
    return jax.shard_map(
        local,
        mesh=mesh,
        in_specs=(
            P(None, ("space", "work")),
            P(None, ("space", "work")),
            P(("space", "work")),
            P(("space", "work")),
            P(("space", "work"), None),
            P(("space", "work"), None),
            P(("space", "work"), None),
            P(("space", "work"), None),
        ),
        out_specs=(
            P(None, ("space", "work")),
            P(None, ("space", "work")),
            P(None, ("space", "work")),
            P(("space", "work")),
        ),
        check_vma=False,
    )
```

```python
import functools
import math

import jax
import jax.numpy as jnp
from jax import lax
from jax.experimental import pallas as pl
from jax.experimental.pallas import tpu as pltpu
from jax.sharding import PartitionSpec as P

STEPS = 2
MESH = pl.DeviceIdType.MESH
NT = (((1,), (1,)), ((), ()))
NN = (((1,), (0,)), ((), ()))
LOG2E = math.log2(math.e)
ROOT_LOG2E = math.sqrt(LOG2E)

star_mass = 0.5
softening = 0.1
time_step = 0.1


def inverse(value):
    guess = pl.reciprocal(value, approx=True)
    return guess * (2.0 - value * guess)


def halves(value):
    high = value.astype(jnp.bfloat16)
    return high, (value - high.astype(jnp.float32)).astype(jnp.bfloat16)


def kernel(
    work, space,
    pos_in, vel_in, mass_in, snd_in, ghost_in, dens_in, dest_in, tiles_in,
    new_pos, new_vel, acc_out, den_out,
    result, pos, vel, mass, snd, ghost, dens, dest_s, tiles_s, dest_v, tiles_v, load_sem,
    spread, spread_rho, cand, factors, totals, weights, gathered, moments, sums,
    sector, fixed, rho, pressure, ghosts_out, ghosts_in, react_out, react_in,
    send_sem, recv_sem, ghost_send, ghost_recv,
):
    tiles = mass.shape[0]
    pairs = dest_v.shape[1]
    ghost_count = ghost.shape[1]
    listed = dens.shape[1]
    unroll, tile_unroll = math.gcd(pairs, 8), math.gcd(tiles, 4)
    loads = []
    for n, (source, target) in enumerate((
        (pos_in, pos), (vel_in, vel), (mass_in, mass), (snd_in, snd), (ghost_in, ghost),
        (dens_in, dens), (dest_in, dest_s), (tiles_in, tiles_s), (dest_in, dest_v),
        (tiles_in, tiles_v),
    )):
        copy = pltpu.make_async_copy(source, target, load_sem.at[n])
        copy.start()
        loads.append(copy)
    me = lax.axis_index("work")
    here = lax.axis_index("space")
    above, below = lax.rem(here + 1, space), lax.rem(here + space - 1, space)

    partners = []
    for s in reversed(range(1, work)):
        partner, digit = 0, 1
        while digit < work:
            partner = partner + digit * (((me // digit) + (s // digit)) % 2)
            digit = 2 * digit
        partners.append(partner)

    barrier = pltpu.get_barrier_semaphore()
    for partner in partners:
        pl.semaphore_signal(barrier, inc=1, device_id={"work": partner}, device_id_type=MESH)
    for z in (above, below):
        pl.semaphore_signal(barrier, inc=1, device_id={"space": z}, device_id_type=MESH)

    def everyone(kind, source, target, own_slot):
        copies = []
        for partner in partners:
            copies.append(pltpu.make_async_remote_copy(
                src_ref=source.at[me] if own_slot else source.at[partner],
                dst_ref=target.at[me],
                send_sem=send_sem.at[kind], recv_sem=recv_sem.at[kind],
                device_id={"work": partner}, device_id_type=MESH,
            ))
        every = target.at[0 : work - 1]
        together = pltpu.make_async_remote_copy(
            src_ref=every, dst_ref=every, send_sem=send_sem.at[kind], recv_sem=recv_sem.at[kind],
            device_id={"work": partners[0]}, device_id_type=MESH,
        )
        return copies, together

    for copy in loads:
        copy.wait()
    masses = mass[...]
    sound2 = snd[...]
    sound = jnp.sqrt(sound2)
    for k in range(3):
        for t in range(tiles):
            result[k, t : t + 1, :] = pos[k : k + 1, 128 * t : 128 * t + 128]
            result[3 + k, t : t + 1, :] = vel[k : k + 1, 128 * t : 128 * t + 128]
    fixed[me, 0] = masses
    fixed[me, 1] = sound
    cand[3, 0:tiles, :] = jnp.log2(masses)
    lanes = lax.broadcasted_iota(jnp.int32, (128, 128), 1)
    owner_hits = (
        lax.broadcasted_iota(jnp.int32, (work * tiles, pairs), 0)
        == dest_v[...] * tiles + tiles_v[1:2, :]
    ).astype(jnp.float32).astype(jnp.bfloat16)
    first_hits = (
        lax.broadcasted_iota(jnp.int32, (tiles, pairs), 0) == tiles_v[0:1, :]
    ).astype(jnp.float32).astype(jnp.bfloat16)

    fixed_copies, fixed_all = everyone(3, fixed, fixed, True)
    sector_copies, sector_all = everyone(0, sector, sector, True)
    rho_copies, rho_all = everyone(1, rho, rho, True)
    react_copies, react_all = everyone(2, react_out, react_in, False)

    def one_step(step, carry):
        positions = [result[k] for k in range(3)]
        velocities = [result[3 + k] for k in range(3)]
        for k in range(3):
            cand[k, 0:tiles, :] = positions[k] * ROOT_LOG2E
            sector[me, k] = positions[k]
            sector[me, 3 + k] = velocities[k]
        for way in range(2):
            rows = [
                cand[k, pl.ds(ghost[way, j], 1), :] for k in range(4) for j in range(ghost_count)
            ]
            ghosts_out[step, way] = jnp.concatenate(rows, axis=0)

        @pl.when(step == 0)
        def _():
            pl.semaphore_wait(barrier, work + 1)

        ghost_copies = []
        for way, z in enumerate((above, below)):
            copy = pltpu.make_async_remote_copy(
                src_ref=ghosts_out.at[step, way], dst_ref=ghosts_in.at[step, way],
                send_sem=ghost_send.at[step, way], recv_sem=ghost_recv.at[step, way],
                device_id={"space": z}, device_id_type=MESH,
            )
            copy.start()
            ghost_copies.append(copy)
        for copy in sector_copies:
            copy.start()

        @pl.when(step == 0)
        def _():
            for copy in fixed_copies:
                copy.start()

        @pl.when(step > 0)
        def _():
            react_all.wait_send()

        def gap2(home, row):
            gaps = [home[k] - row[k] for k in range(3)]
            return gaps[0] * gaps[0] + gaps[1] * gaps[1] + gaps[2] * gaps[2]

        def wide_row(number):
            return [
                jnp.broadcast_to(cand[k, pl.ds(number, 1), :], (32, 128)) for k in range(4)
            ]

        planes = positions + velocities + [sound]
        blank = jnp.zeros((128 - tiles * len(planes), 128), jnp.float32)
        columns = jnp.concatenate(planes + [blank], axis=0).T

        for t in range(tiles):
            for q in range(len(planes)):
                c = q * tiles + t
                spread[t, q] = jnp.broadcast_to(columns[:, c : c + 1], (128, 128))
        for t in range(tiles):
            row = [jnp.broadcast_to(cand[k, t : t + 1, :], (32, 128)) for k in range(4)]
            for i in range(0, 128, 32):
                home = [spread[t, k, i : i + 32, :] * ROOT_LOG2E for k in range(3)]
                totals[t, i : i + 32, :] = jnp.exp2(row[3] - gap2(home, row))
        for copy in ghost_copies:
            copy.wait_recv()
        for way in range(2):
            first = tiles + way * ghost_count
            for k in range(4):
                cand[k, first : first + ghost_count, :] = ghosts_in[
                    step, way, k * ghost_count : (k + 1) * ghost_count, :
                ]

        def density_of(first, carry):
            for t in [first * tile_unroll + u for u in range(tile_unroll)]:
                rows = [wide_row(dens[t, c]) for c in range(listed)]
                parts = []
                for i in range(0, 128, 32):
                    home = [spread[t, k, i : i + 32, :] * ROOT_LOG2E for k in range(3)]
                    part = totals[t, i : i + 32, :]
                    for row in rows:
                        part = part + jnp.exp2(row[3] - gap2(home, row))
                    parts.append(jnp.sum(part, axis=1, keepdims=True))
                spread_rho[t, 0] = jnp.broadcast_to(jnp.concatenate(parts, axis=0), (128, 128))
            return carry

        lax.fori_loop(0, tiles // tile_unroll, density_of, 0)
        columns = jnp.zeros((128, 128), jnp.float32)
        for t in range(tiles):
            columns = jnp.where(lanes == t, spread_rho[t, 0], columns)
        density = columns.T[0:tiles, :]
        result[9] = density
        rho[me] = density
        for copy in rho_copies:
            copy.start()

        for t in range(tiles):
            speed = spread[t, 6]
            spread_rho[t, 1] = speed * speed * inverse(spread_rho[t, 0])

        sector_all.wait_recv()

        @pl.when(step == 0)
        def _():
            fixed_all.wait_recv()

        def pair_factors(turn, carry):
            for u in range(unroll):
                p = turn * unroll + u
                a, owner, b = tiles_s[0, p], dest_s[0, p], tiles_s[1, p]
                row = [sector[owner, k, pl.ds(b, 1), :] for k in range(6)]
                row.append(fixed[owner, 1, pl.ds(b, 1), :])
                kept = [sector[me, k, pl.ds(a, 1), :] for k in range(3)]
                kept.append(fixed[me, 0, pl.ds(a, 1), :])
                kept = kept + row[0:3] + [fixed[owner, 0, pl.ds(b, 1), :]]
                row = [jnp.broadcast_to(value, (32, 128)) for value in row]
                for i in range(0, 128, 32):
                    home = [spread[a, k, i : i + 32, :] for k in range(7)]
                    gaps = [home[k] - row[k] for k in range(3)]
                    distance2 = gaps[0] * gaps[0] + gaps[1] * gaps[1] + gaps[2] * gaps[2]
                    approach = (home[3] - row[3]) * gaps[0]
                    approach = approach + (home[4] - row[4]) * gaps[1]
                    approach = approach + (home[5] - row[5]) * gaps[2]
                    closing = jnp.minimum(approach * inverse(distance2 + 0.01), 0.0)
                    twice = jnp.exp2(1.0 - distance2 * LOG2E)
                    factors[p, 0, i : i + 32, :] = twice
                    factors[p, 1, i : i + 32, :] = (
                        twice * closing * (4.0 * closing - (home[6] + row[6]))
                    )
                for k in range(8):
                    gathered[k, pl.ds(p, 1), :] = kept[k]
            return carry

        lax.fori_loop(0, pairs // unroll, pair_factors, 0)
        for side in range(2):
            mass_rows = gathered[4 * side + 3]
            for k in range(4):
                value = mass_rows if k == 3 else mass_rows * gathered[4 * side + k]
                for g in range(3):
                    piece = value.astype(jnp.bfloat16).astype(jnp.float32)
                    value = value - piece
                    moments[side, pl.ds((4 * g + k) * pairs, pairs), :] = piece
        rho_all.wait_recv()
        for w in range(work):
            pressure[w] = fixed[w, 1] * fixed[w, 1] / rho[w]

        def own_moments(side, p):
            rows = moments[side, pl.ds(p, 12, stride=pairs), :].astype(jnp.bfloat16)
            return jnp.concatenate([rows, rows], axis=1)

        def gains(side):
            moved = [
                sums[side, pl.ds(k * pairs, pairs), :]
                + sums[side, pl.ds((4 + k) * pairs, pairs), :]
                + sums[side, pl.ds((8 + k) * pairs, pairs), :]
                for k in range(4)
            ]
            return [gathered[4 * side + k] * moved[3] - moved[k] for k in range(3)]

        def pair_weights(turn, carry):
            results = []
            for u in range(unroll):
                p = turn * unroll + u
                a, owner, b = tiles_s[0, p], dest_s[0, p], tiles_s[1, p]
                row_rho = jnp.broadcast_to(rho[owner, pl.ds(b, 1), :], (32, 128))
                row_pressure = jnp.broadcast_to(pressure[owner, pl.ds(b, 1), :], (32, 128))
                parts = []
                for i in range(0, 128, 32):
                    own = pl.ds(i, 32)
                    weight = factors[p, 0, own, :] * (spread_rho[a, 1, own, :] + row_pressure)
                    weight = weight + factors[p, 1, own, :] * inverse(
                        spread_rho[a, 0, own, :] + row_rho
                    )
                    high, low = halves(weight)
                    weights[p, 0, own, :] = high
                    weights[p, 1, own, :] = low
                    parts.append((high, low))
                stacked = jnp.concatenate([h for h, _ in parts] + [l for _, l in parts], axis=0)
                results.append((p, lax.dot_general(
                    own_moments(0, p), stacked, NN, preferred_element_type=jnp.float32
                )))
            for p, moved in results:
                sums[1, pl.ds(p, 12, stride=pairs), :] = moved
            return carry

        def first_sums(turn, carry):
            results = []
            for u in range(unroll):
                p = turn * unroll + u
                results.append((p, lax.dot_general(
                    own_moments(1, p),
                    jnp.concatenate([weights[p, 0], weights[p, 1]], axis=1),
                    NT, preferred_element_type=jnp.float32,
                )))
            for p, moved in results:
                sums[0, pl.ds(p, 12, stride=pairs), :] = moved
            return carry

        lax.fori_loop(0, pairs // unroll, pair_weights, 0)
        reaction = added(owner_hits, gains(1))
        for k in range(3):
            for w in range(work):
                react_out[w, k] = reaction[w * tiles : (w + 1) * tiles, 128 * k : 128 * k + 128]
        for copy in react_copies:
            copy.start()
        lax.fori_loop(0, pairs // unroll, first_sums, 0)
        radius2 = positions[0] * positions[0] + positions[1] * positions[1]
        radius2 = radius2 + positions[2] * positions[2] + softening
        pull = -star_mass / (radius2 * jnp.sqrt(radius2))
        acceleration = []
        gain = added(first_hits, gains(0))
        for k in range(3):
            own = gain[:, 128 * k : 128 * k + 128]
            acceleration.append(own + pull * positions[k] + react_out[me, k])
        sector_all.wait_send()
        rho_all.wait_send()
        for copy in ghost_copies:
            copy.wait_send()
        react_all.wait_recv()
        for partner in partners:
            for k in range(3):
                acceleration[k] = acceleration[k] + react_in[partner, k]
        for k in range(3):
            velocity = velocities[k] + time_step * acceleration[k]
            result[k] = positions[k] + time_step * velocity
            result[3 + k] = velocity
            result[6 + k] = acceleration[k]
        return carry

    lax.fori_loop(0, STEPS, one_step, 0)
    react_all.wait_send()
    fixed_all.wait_send()
    den_out[...] = result[9]
    for n, out in enumerate((new_pos, new_vel, acc_out)):
        for k in range(3):
            for t in range(tiles):
                out[k : k + 1, 128 * t : 128 * t + 128] = result[3 * n + k, t : t + 1, :]


def added(hits, values):
    value = jnp.concatenate(values, axis=1)
    pieces = []
    for _ in range(3):
        piece = value.astype(jnp.bfloat16)
        value = value - piece.astype(jnp.float32)
        pieces.append(piece)
    return lax.dot_general(
        jnp.concatenate([hits] * 3, axis=1), jnp.concatenate(pieces, axis=0), NN,
        preferred_element_type=jnp.float32,
    )


def hand_on(*refs):
    count = len(refs) // 2
    copies = [
        pltpu.make_async_copy(refs[n], refs[count + n], refs[-1].at[n]) for n in range(count)
    ]
    for copy in copies:
        copy.start()
    for copy in copies:
        copy.wait()


def local(positions, velocities, masses, sound2, ghost_list, dens_list, pair_dest, pair_tiles):
    work, space = lax.axis_size("work"), lax.axis_size("space")
    particles = positions.shape[1]
    tiles = particles // 128
    pairs = pair_dest.shape[0]
    ghosts = ghost_list.shape[0]
    vmem = pl.BlockSpec(memory_space=pltpu.VMEM)
    f32 = jnp.float32
    i32 = jnp.int32
    wide = jax.ShapeDtypeStruct((3, particles), f32)
    shapes = (wide, wide, wide, jax.ShapeDtypeStruct((tiles, 128), f32))
    results = pl.pallas_call(
        functools.partial(kernel, work, space),
        out_shape=shapes,
        in_specs=[pl.BlockSpec(memory_space=pltpu.HBM)] * 8,
        out_specs=(vmem,) * 4,
        scratch_shapes=[
            pltpu.VMEM((10, tiles, 128), f32),
            pltpu.VMEM((3, particles), f32),
            pltpu.VMEM((3, particles), f32),
            pltpu.VMEM((tiles, 128), f32),
            pltpu.VMEM((tiles, 128), f32),
            pltpu.SMEM((2, ghosts), i32),
            pltpu.SMEM(dens_list.shape, i32),
            pltpu.SMEM((1, pairs), i32),
            pltpu.SMEM((2, pairs), i32),
            pltpu.VMEM((1, pairs), i32),
            pltpu.VMEM((2, pairs), i32),
            pltpu.SemaphoreType.DMA((10,)),
            pltpu.VMEM((tiles, 7, 128, 128), f32),
            pltpu.VMEM((tiles, 2, 128, 128), f32),
            pltpu.VMEM((4, tiles + 2 * ghosts, 128), f32),
            pltpu.VMEM((pairs, 2, 128, 128), f32),
            pltpu.VMEM((tiles, 128, 128), f32),
            pltpu.VMEM((pairs, 2, 128, 128), jnp.bfloat16),
            pltpu.VMEM((8, pairs, 128), f32),
            pltpu.VMEM((2, 12 * pairs, 128), f32),
            pltpu.VMEM((2, 12 * pairs, 128), f32),
            pltpu.VMEM((work, 6, tiles, 128), f32),
            pltpu.VMEM((work, 2, tiles, 128), f32),
            pltpu.VMEM((work, tiles, 128), f32),
            pltpu.VMEM((work, tiles, 128), f32),
            pltpu.VMEM((STEPS, 2, 4 * ghosts, 128), f32),
            pltpu.VMEM((STEPS, 2, 4 * ghosts, 128), f32),
            pltpu.VMEM((work, 3, tiles, 128), f32),
            pltpu.VMEM((work, 3, tiles, 128), f32),
            pltpu.SemaphoreType.DMA((4,)),
            pltpu.SemaphoreType.DMA((4,)),
            pltpu.SemaphoreType.DMA((STEPS, 2)),
            pltpu.SemaphoreType.DMA((STEPS, 2)),
        ],
        compiler_params=pltpu.CompilerParams(
            collective_id=0, has_side_effects=True, vmem_limit_bytes=63 * 1024 * 1024
        ),
        name="leapfrog",
    )(
        positions, velocities, masses.reshape(tiles, 128), sound2.reshape(tiles, 128),
        ghost_list.T, dens_list, pair_dest.T, pair_tiles.T,
    )
    hbm = pl.BlockSpec(memory_space=pltpu.HBM)
    outs = pl.pallas_call(
        hand_on,
        out_shape=shapes,
        in_specs=[hbm] * 4,
        out_specs=(hbm,) * 4,
        scratch_shapes=[pltpu.SemaphoreType.DMA((4,))],
        compiler_params=pltpu.CompilerParams(vmem_limit_bytes=63 * 1024 * 1024),
        name="hand_on",
    )(*results)
    return outs[0], outs[1], outs[2], outs[3].reshape(particles)


def solution(mesh):
    return jax.shard_map(
        local,
        mesh=mesh,
        in_specs=(
            P(None, ("space", "work")),
            P(None, ("space", "work")),
            P(("space", "work")),
            P(("space", "work")),
            P(("space", "work"), None),
            P(("space", "work"), None),
            P(("space", "work"), None),
            P(("space", "work"), None),
        ),
        out_specs=(
            P(None, ("space", "work")),
            P(None, ("space", "work")),
            P(None, ("space", "work")),
            P(("space", "work")),
        ),
        check_vma=False,
    )
```

```python
import functools
import math

import jax
import jax.numpy as jnp
from jax import lax
from jax.experimental import pallas as pl
from jax.experimental.pallas import tpu as pltpu
from jax.sharding import PartitionSpec as P

STEPS = 2
MESH = pl.DeviceIdType.MESH
NT = (((1,), (1,)), ((), ()))
NN = (((1,), (0,)), ((), ()))
LOG2E = math.log2(math.e)
ROOT_LOG2E = math.sqrt(LOG2E)

star_mass = 0.5
softening = 0.1
time_step = 0.1


def inverse(value):
    guess = pl.reciprocal(value, approx=True)
    return guess * (2.0 - value * guess)


def halves(value):
    high = value.astype(jnp.bfloat16)
    return high, (value - high.astype(jnp.float32)).astype(jnp.bfloat16)


def kernel(
    work, space,
    pos_in, vel_in, mass_in, snd_in, ghost_in, dens_in, dest_in, tiles_in,
    result,
    pos, vel, mass, snd, ghost, dens, dest_s, tiles_s, dest_v, tiles_v, load_sem,
    spread, spread_rho, cand, factors, totals, weights, gathered, moments, sums,
    sector, fixed, rho, pressure, ghosts_out, ghosts_in, react_out, react_in,
    send_sem, recv_sem, ghost_send, ghost_recv,
):
    tiles = mass.shape[0]
    pairs = dest_v.shape[1]
    ghost_count = ghost.shape[1]
    listed = dens.shape[1]
    unroll, tile_unroll = math.gcd(pairs, 16), math.gcd(tiles, 8)
    me = lax.axis_index("work")
    here = lax.axis_index("space")
    above, below = lax.rem(here + 1, space), lax.rem(here + space - 1, space)
    partners = []
    for s in reversed(range(1, work)):
        partner, digit = 0, 1
        while digit < work:
            partner = partner + digit * (((me // digit) + (s // digit)) % 2)
            digit = 2 * digit
        partners.append(partner)

    barrier = pltpu.get_barrier_semaphore()
    for partner in partners:
        pl.semaphore_signal(barrier, inc=1, device_id={"work": partner}, device_id_type=MESH)
    for z in (above, below):
        pl.semaphore_signal(barrier, inc=1, device_id={"space": z}, device_id_type=MESH)

    loads = []
    for n, (source, target) in enumerate((
        (pos_in, pos), (vel_in, vel), (mass_in, mass), (snd_in, snd), (ghost_in, ghost),
        (dens_in, dens), (dest_in, dest_s), (tiles_in, tiles_s), (dest_in, dest_v),
        (tiles_in, tiles_v),
    )):
        copy = pltpu.make_async_copy(source, target, load_sem.at[n])
        copy.start()
        loads.append(copy)

    def everyone(kind, source, target, own_slot):
        copies = []
        for partner in partners:
            copies.append(pltpu.make_async_remote_copy(
                src_ref=source.at[me] if own_slot else source.at[partner],
                dst_ref=target.at[me],
                send_sem=send_sem.at[kind], recv_sem=recv_sem.at[kind],
                device_id={"work": partner}, device_id_type=MESH,
            ))
        every = target.at[0 : work - 1]
        together = pltpu.make_async_remote_copy(
            src_ref=every, dst_ref=every, send_sem=send_sem.at[kind], recv_sem=recv_sem.at[kind],
            device_id={"work": partners[0]}, device_id_type=MESH,
        )
        return copies, together

    for copy in loads:
        copy.wait()
    masses = mass[...]
    sound2 = snd[...]
    sound = jnp.sqrt(sound2)
    for k in range(3):
        for t in range(tiles):
            result[k, t : t + 1, :] = pos[k : k + 1, 128 * t : 128 * t + 128]
            result[3 + k, t : t + 1, :] = vel[k : k + 1, 128 * t : 128 * t + 128]
    fixed[me, 0] = masses
    fixed[me, 1] = sound
    cand[3, 0:tiles, :] = jnp.log2(masses)
    lanes = lax.broadcasted_iota(jnp.int32, (128, 128), 1)
    owner_hits = (
        lax.broadcasted_iota(jnp.int32, (work * tiles, pairs), 0)
        == dest_v[...] * tiles + tiles_v[1:2, :]
    ).astype(jnp.float32).astype(jnp.bfloat16)
    first_hits = (
        lax.broadcasted_iota(jnp.int32, (tiles, pairs), 0) == tiles_v[0:1, :]
    ).astype(jnp.float32).astype(jnp.bfloat16)

    fixed_copies, fixed_all = everyone(3, fixed, fixed, True)
    sector_copies, sector_all = everyone(0, sector, sector, True)
    rho_copies, rho_all = everyone(1, rho, rho, True)
    react_copies, react_all = everyone(2, react_out, react_in, False)

    columns = jnp.concatenate([sound, jnp.zeros((128 - tiles, 128), jnp.float32)], axis=0).T
    for t in range(tiles):
        spread[t, 6] = jnp.broadcast_to(columns[:, t : t + 1], (128, 128))

    def one_step(step, carry):
        positions = [result[k] for k in range(3)]
        velocities = [result[3 + k] for k in range(3)]
        for k in range(3):
            cand[k, 0:tiles, :] = positions[k] * ROOT_LOG2E
            sector[me, k] = positions[k]
            sector[me, 3 + k] = velocities[k]
        for way in range(2):
            rows = [
                cand[k, pl.ds(ghost[way, j], 1), :] for k in range(4) for j in range(ghost_count)
            ]
            ghosts_out[step, way] = jnp.concatenate(rows, axis=0)

        @pl.when(step == 0)
        def _():
            pl.semaphore_wait(barrier, work + 1)

        ghost_copies = []
        for way, z in enumerate((above, below)):
            copy = pltpu.make_async_remote_copy(
                src_ref=ghosts_out.at[step, way], dst_ref=ghosts_in.at[step, way],
                send_sem=ghost_send.at[step, way], recv_sem=ghost_recv.at[step, way],
                device_id={"space": z}, device_id_type=MESH,
            )
            copy.start()
            ghost_copies.append(copy)
        for copy in sector_copies:
            copy.start()

        @pl.when(step == 0)
        def _():
            for copy in fixed_copies:
                copy.start()

        @pl.when(step > 0)
        def _():
            react_all.wait_send()

        def gap2(home, row):
            gaps = [home[k] - row[k] for k in range(3)]
            return gaps[0] * gaps[0] + gaps[1] * gaps[1] + gaps[2] * gaps[2]

        def wide_row(number):
            return [
                jnp.broadcast_to(cand[k, pl.ds(number, 1), :], (32, 128)) for k in range(4)
            ]

        planes = positions + velocities
        blank = jnp.zeros((128 - tiles * len(planes), 128), jnp.float32)
        columns = jnp.concatenate(planes + [blank], axis=0).T

        for t in range(tiles):
            for q in range(len(planes)):
                c = q * tiles + t
                spread[t, q] = jnp.broadcast_to(columns[:, c : c + 1], (128, 128))
        for t in range(tiles):
            row = [jnp.broadcast_to(cand[k, t : t + 1, :], (32, 128)) for k in range(4)]
            for i in range(0, 128, 32):
                home = [spread[t, k, i : i + 32, :] * ROOT_LOG2E for k in range(3)]
                totals[t, i : i + 32, :] = jnp.exp2(row[3] - gap2(home, row))
        for copy in ghost_copies:
            copy.wait_recv()
        for way in range(2):
            first = tiles + way * ghost_count
            for k in range(4):
                cand[k, first : first + ghost_count, :] = ghosts_in[
                    step, way, k * ghost_count : (k + 1) * ghost_count, :
                ]

        def density_of(first, carry):
            for t in [first * tile_unroll + u for u in range(tile_unroll)]:
                rows = [wide_row(dens[t, c]) for c in range(listed)]
                parts = []
                for i in range(0, 128, 32):
                    home = [spread[t, k, i : i + 32, :] * ROOT_LOG2E for k in range(3)]
                    part = totals[t, i : i + 32, :]
                    for row in rows:
                        part = part + jnp.exp2(row[3] - gap2(home, row))
                    parts.append(jnp.sum(part, axis=1, keepdims=True))
                spread_rho[t, 0] = jnp.broadcast_to(jnp.concatenate(parts, axis=0), (128, 128))
            return carry

        lax.fori_loop(0, tiles // tile_unroll, density_of, 0)
        columns = jnp.zeros((128, 128), jnp.float32)
        for t in range(tiles):
            columns = jnp.where(lanes == t, spread_rho[t, 0], columns)
        density = columns.T[0:tiles, :]
        result[9] = density
        rho[me] = density
        for copy in rho_copies:
            copy.start()

        for t in range(tiles):
            speed = spread[t, 6]
            spread_rho[t, 1] = speed * speed * inverse(spread_rho[t, 0])

        sector_all.wait_recv()

        @pl.when(step == 0)
        def _():
            fixed_all.wait_recv()

        def pair_factors(turn, carry):
            for u in range(unroll):
                p = turn * unroll + u
                a, owner, b = tiles_s[0, p], dest_s[0, p], tiles_s[1, p]
                row = [sector[owner, k, pl.ds(b, 1), :] for k in range(6)]
                row.append(fixed[owner, 1, pl.ds(b, 1), :])
                kept = [sector[me, k, pl.ds(a, 1), :] for k in range(3)]
                kept.append(fixed[me, 0, pl.ds(a, 1), :])
                kept = kept + row[0:3] + [fixed[owner, 0, pl.ds(b, 1), :]]
                row = [jnp.broadcast_to(value, (32, 128)) for value in row]
                for i in range(0, 128, 32):
                    home = [spread[a, k, i : i + 32, :] for k in range(7)]
                    gaps = [home[k] - row[k] for k in range(3)]
                    distance2 = gaps[0] * gaps[0] + gaps[1] * gaps[1] + gaps[2] * gaps[2]
                    approach = (home[3] - row[3]) * gaps[0]
                    approach = approach + (home[4] - row[4]) * gaps[1]
                    approach = approach + (home[5] - row[5]) * gaps[2]
                    closing = jnp.minimum(approach * inverse(distance2 + 0.01), 0.0)
                    twice = jnp.exp2(1.0 - distance2 * LOG2E)
                    factors[p, 0, i : i + 32, :] = twice
                    factors[p, 1, i : i + 32, :] = (
                        twice * closing * (4.0 * closing - (home[6] + row[6]))
                    )
                for k in range(8):
                    gathered[k, pl.ds(p, 1), :] = kept[k]
            return carry

        lax.fori_loop(0, pairs // unroll, pair_factors, 0)
        for side in range(2):
            mass_rows = gathered[4 * side + 3]
            for k in range(4):
                value = mass_rows if k == 3 else mass_rows * gathered[4 * side + k]
                for g in range(3):
                    piece = value.astype(jnp.bfloat16).astype(jnp.float32)
                    value = value - piece
                    moments[side, pl.ds((4 * g + k) * pairs, pairs), :] = piece
        rho_all.wait_recv()
        for w in range(work):
            pressure[w] = fixed[w, 1] * fixed[w, 1] / rho[w]

        def own_moments(side, p):
            rows = moments[side, pl.ds(p, 12, stride=pairs), :].astype(jnp.bfloat16)
            return jnp.concatenate([rows, rows], axis=1)

        def gains(side):
            moved = [
                sums[side, pl.ds(k * pairs, pairs), :]
                + sums[side, pl.ds((4 + k) * pairs, pairs), :]
                + sums[side, pl.ds((8 + k) * pairs, pairs), :]
                for k in range(4)
            ]
            return [gathered[4 * side + k] * moved[3] - moved[k] for k in range(3)]

        def pair_weights(turn, carry):
            results = []
            for u in range(unroll):
                p = turn * unroll + u
                a, owner, b = tiles_s[0, p], dest_s[0, p], tiles_s[1, p]
                row_rho = jnp.broadcast_to(rho[owner, pl.ds(b, 1), :], (32, 128))
                row_pressure = jnp.broadcast_to(pressure[owner, pl.ds(b, 1), :], (32, 128))
                parts = []
                for i in range(0, 128, 32):
                    own = pl.ds(i, 32)
                    weight = factors[p, 0, own, :] * (spread_rho[a, 1, own, :] + row_pressure)
                    weight = weight + factors[p, 1, own, :] * inverse(
                        spread_rho[a, 0, own, :] + row_rho
                    )
                    high, low = halves(weight)
                    weights[p, 0, own, :] = high
                    weights[p, 1, own, :] = low
                    parts.append((high, low))
                stacked = jnp.concatenate([h for h, _ in parts] + [l for _, l in parts], axis=0)
                results.append((p, lax.dot_general(
                    own_moments(0, p), stacked, NN, preferred_element_type=jnp.float32
                )))
            for p, moved in results:
                sums[1, pl.ds(p, 12, stride=pairs), :] = moved
            return carry

        def first_sums(turn, carry):
            results = []
            for u in range(unroll):
                p = turn * unroll + u
                results.append((p, lax.dot_general(
                    own_moments(1, p),
                    jnp.concatenate([weights[p, 0], weights[p, 1]], axis=1),
                    NT, preferred_element_type=jnp.float32,
                )))
            for p, moved in results:
                sums[0, pl.ds(p, 12, stride=pairs), :] = moved
            return carry

        lax.fori_loop(0, pairs // unroll, pair_weights, 0)
        reaction = added(owner_hits, gains(1))
        for k in range(3):
            for w in range(work):
                react_out[w, k] = reaction[w * tiles : (w + 1) * tiles, 128 * k : 128 * k + 128]
        for copy in react_copies:
            copy.start()
        lax.fori_loop(0, pairs // unroll, first_sums, 0)
        radius2 = positions[0] * positions[0] + positions[1] * positions[1]
        radius2 = radius2 + positions[2] * positions[2] + softening
        pull = -star_mass / (radius2 * jnp.sqrt(radius2))
        acceleration = []
        gain = added(first_hits, gains(0))
        for k in range(3):
            own = gain[:, 128 * k : 128 * k + 128]
            acceleration.append(own + pull * positions[k] + react_out[me, k])
        sector_all.wait_send()
        rho_all.wait_send()
        for copy in ghost_copies:
            copy.wait_send()
        react_all.wait_recv()
        for partner in partners:
            for k in range(3):
                acceleration[k] = acceleration[k] + react_in[partner, k]
        for k in range(3):
            velocity = velocities[k] + time_step * acceleration[k]
            result[k] = positions[k] + time_step * velocity
            result[3 + k] = velocity
            result[6 + k] = acceleration[k]
        return carry

    lax.fori_loop(0, STEPS, one_step, 0)
    react_all.wait_send()
    fixed_all.wait_send()


def added(hits, values):
    value = jnp.concatenate(values, axis=1)
    pieces = []
    for _ in range(3):
        piece = value.astype(jnp.bfloat16)
        value = value - piece.astype(jnp.float32)
        pieces.append(piece)
    return lax.dot_general(
        jnp.concatenate([hits] * 3, axis=1), jnp.concatenate(pieces, axis=0), NN,
        preferred_element_type=jnp.float32,
    )


def unpack(result, new_pos, new_vel, acc_out, den_out):
    den_out[...] = result[9]
    for n, out in enumerate((new_pos, new_vel, acc_out)):
        for k in range(3):
            for t in range(den_out.shape[0]):
                out[k : k + 1, 128 * t : 128 * t + 128] = result[3 * n + k, t : t + 1, :]


def local(positions, velocities, masses, sound2, ghost_list, dens_list, pair_dest, pair_tiles):
    work, space = lax.axis_size("work"), lax.axis_size("space")
    particles = positions.shape[1]
    tiles = particles // 128
    pairs = pair_dest.shape[0]
    ghosts = ghost_list.shape[0]
    vmem = pl.BlockSpec(memory_space=pltpu.VMEM)
    f32 = jnp.float32
    i32 = jnp.int32
    wide = jax.ShapeDtypeStruct((3, particles), f32)
    shapes = (wide, wide, wide, jax.ShapeDtypeStruct((tiles, 128), f32))
    packed = pl.pallas_call(
        functools.partial(kernel, work, space),
        out_shape=jax.ShapeDtypeStruct((10, tiles, 128), f32),
        in_specs=[pl.BlockSpec(memory_space=pltpu.HBM)] * 8,
        out_specs=vmem,
        scratch_shapes=[
            pltpu.VMEM((3, particles), f32),
            pltpu.VMEM((3, particles), f32),
            pltpu.VMEM((tiles, 128), f32),
            pltpu.VMEM((tiles, 128), f32),
            pltpu.SMEM((2, ghosts), i32),
            pltpu.SMEM(dens_list.shape, i32),
            pltpu.SMEM((1, pairs), i32),
            pltpu.SMEM((2, pairs), i32),
            pltpu.VMEM((1, pairs), i32),
            pltpu.VMEM((2, pairs), i32),
            pltpu.SemaphoreType.DMA((10,)),
            pltpu.VMEM((tiles, 7, 128, 128), f32),
            pltpu.VMEM((tiles, 2, 128, 128), f32),
            pltpu.VMEM((4, tiles + 2 * ghosts, 128), f32),
            pltpu.VMEM((pairs, 2, 128, 128), f32),
            pltpu.VMEM((tiles, 128, 128), f32),
            pltpu.VMEM((pairs, 2, 128, 128), jnp.bfloat16),
            pltpu.VMEM((8, pairs, 128), f32),
            pltpu.VMEM((2, 12 * pairs, 128), f32),
            pltpu.VMEM((2, 12 * pairs, 128), f32),
            pltpu.VMEM((work, 6, tiles, 128), f32),
            pltpu.VMEM((work, 2, tiles, 128), f32),
            pltpu.VMEM((work, tiles, 128), f32),
            pltpu.VMEM((work, tiles, 128), f32),
            pltpu.VMEM((STEPS, 2, 4 * ghosts, 128), f32),
            pltpu.VMEM((STEPS, 2, 4 * ghosts, 128), f32),
            pltpu.VMEM((work, 3, tiles, 128), f32),
            pltpu.VMEM((work, 3, tiles, 128), f32),
            pltpu.SemaphoreType.DMA((4,)),
            pltpu.SemaphoreType.DMA((4,)),
            pltpu.SemaphoreType.DMA((STEPS, 2)),
            pltpu.SemaphoreType.DMA((STEPS, 2)),
        ],
        compiler_params=pltpu.CompilerParams(
            collective_id=0, has_side_effects=True, vmem_limit_bytes=63 * 1024 * 1024
        ),
        name="leapfrog",
    )(
        positions, velocities, masses.reshape(tiles, 128), sound2.reshape(tiles, 128),
        ghost_list.T, dens_list, pair_dest.T, pair_tiles.T,
    )
    outs = pl.pallas_call(
        unpack,
        out_shape=shapes,
        in_specs=[vmem],
        out_specs=(vmem,) * 4,
        name="unpack",
    )(packed)
    return outs[0], outs[1], outs[2], outs[3].reshape(particles)


def solution(mesh):
    return jax.shard_map(
        local,
        mesh=mesh,
        in_specs=(
            P(None, ("space", "work")),
            P(None, ("space", "work")),
            P(("space", "work")),
            P(("space", "work")),
            P(("space", "work"), None),
            P(("space", "work"), None),
            P(("space", "work"), None),
            P(("space", "work"), None),
        ),
        out_specs=(
            P(None, ("space", "work")),
            P(None, ("space", "work")),
            P(None, ("space", "work")),
            P(("space", "work")),
        ),
        check_vma=False,
    )
```
